512 devices in a mesh: seq: 64 (over z, y), head: 8 (over x, core).
Axes of the slice: x: 4, y: 8, z: 8, core: 2. Of those that a mesh axis runs over, the one named last changes fastest.
Arguments:
- query: bfloat16 [16384, 3072], P('seq', 'head'), may hold values from -120 to 120
- keys: bfloat16 [16384, 3072], P('seq', 'head'), may hold values from -4.1 to 4.1
- values: bfloat16 [16384, 3072], P('seq', 'head'), may hold values from -6 to 6
- shot_ids: int32 [16384], replicated, may hold values from 0 to 31, never falling along the last dimension, each value on 1 to 1025 neighbouring positions
- routes: int32 [256, 8], replicated, may hold values from 0 to 255, as said below
- out_weight: bfloat16 [3072, 3072], P('head'), may hold values from -0.15625 to 0.15625
Outputs:
- mixed_out: bfloat16 [16384, 3072], P('seq', 'head')
The draws below stay inside these ranges and needn't reach their ends.
Inputs may be any that keep to these rules, and one draw needn't show every extreme that they name: `shot_ids`: shots are runs of equal numbers that never fall, each of 1 to 1025 tokens, one exactly 1025. The 8 routes of a query stretch name different stretches. Over the query stretches of one seq index (aligned blocks of 4 rows), the routes name at most 1 stretches of any one seq index's block of 4 stretches, all different, and exactly 1 for some block in every draw.
All inputs are finite; a program needn't handle non-finite values.
Results may differ from the reference program's by a relative error of at most 0.017.
Values may be sent and summed in bfloat16 or wider, within the bound.
A program may use at most 128 MiB of HBM per device.

```python
import math
import jax
import jax.numpy as jnp
import numpy as np
from jax import lax

H = 24
HEAD_DIM = 128
STRETCH = 64
K = 8
TOK_DEV = 256
TOKENS = 16384
STRETCHES = 256
SHOT_MOST = 1025
SHOTS = 32
CAP = 1
GROUPS = 8


def shared_rows(key):
    return jnp.clip(jax.random.normal(key, (TOKENS, H * HEAD_DIM), jnp.float32), -4.0, 4.0)


def draw_query(key, part):
    key = jax.random.fold_in(key, 3)
    own = jnp.clip(jax.random.normal(key, (TOKENS, H * HEAD_DIM), jnp.float32), -4.0, 4.0)
    return own.astype(jnp.bfloat16)


def draw_keys(key, part):
    shared = shared_rows(key)
    return shared.astype(jnp.bfloat16)


def draw_routes(key, part):
    key = jax.random.fold_in(key, 7)
    devices = TOKENS // TOK_DEV
    per_device = TOK_DEV // STRETCH
    total = per_device * K
    groups = (total + CAP - 1) // CAP
    owner_keys = jax.random.split(jax.random.fold_in(key, 1), devices)
    owners = jax.vmap(lambda single: jax.random.permutation(single, devices)[:groups])(owner_keys)
    stretch_keys = jax.random.split(jax.random.fold_in(key, 2), devices * groups)
    picks = jax.vmap(lambda single: jax.random.permutation(single, per_device)[:CAP])(stretch_keys)
    picks = picks.reshape(devices, groups * CAP)[:, :total]
    slot_group = jnp.arange(total) // CAP
    owner_slots = owners[:, slot_group]
    chosen = owner_slots * per_device + picks
    return chosen.reshape(devices * per_device, K).astype(jnp.int32)


def strengthened(drawn, own_key, source, target, shards_of, factor):
    owner, partner = [(jnp.arange(drawn.shape[position]) // (drawn.shape[position] // shards_of)).reshape([-1 if axis == position else 1 for axis in range(drawn.ndim)]) for position in (source, target)]
    chosen = jax.random.permutation(own_key, shards_of)[partner]
    strong = (owner == chosen) | (owner == (partner + shards_of // 2) % shards_of)
    return jnp.where(strong, factor * drawn, drawn)


def shard_levels(stream_key, dims, cuts, smallest, high):
    loudness = 1.0
    for axis_at, blocks in cuts:
        draws = jax.random.uniform(jax.random.fold_in(jax.random.fold_in(stream_key, 6), axis_at), (blocks,), jnp.float32, smallest / len(cuts), high / len(cuts))
        loudness = loudness * jnp.repeat(jnp.exp(draws), dims[axis_at] // blocks).reshape((-1,) + (1,) * (len(dims) - 1 - axis_at))
    return loudness


def length_profile(number_of, total, reach, lean):
    weights = [(1 << 20) // math.isqrt(grade ** lean) + 1 for grade in range(2, number_of + 1)]
    rest, holding = total - reach - (number_of - 1), [1] * (number_of - 1)
    while rest > 0:
        movable = [i for i in range(number_of - 1) if holding[i] < reach]
        whole, budget = sum([weights[i] for i in movable]), rest
        for i in movable:
            addition = min(reach - holding[i], max(1, budget * weights[i] // whole), rest)
            holding[i] = holding[i] + addition
            rest = rest - addition
    return np.array([reach] + holding)


def uneven(stream_key, count, total, bound, skew):
    if count == 2:
        one = jax.random.randint(stream_key, (), max(1, total - bound), min(bound, total - 1) + 1)
        return jnp.stack([one, total - one])
    tallies = jnp.asarray(length_profile(count, total, bound, skew), jnp.int32)
    pairs = (count - 1) // 2
    source_of, sink = tallies[1:1 + 2 * pairs:2], tallies[2:2 + 2 * pairs:2]
    slack = jnp.minimum(source_of - 1, bound - sink)
    moved = jax.random.randint(jax.random.fold_in(stream_key, 1), (pairs,), 0, 1 << 20) % (slack + 1)
    tallies = tallies.at[1:1 + 2 * pairs:2].set(source_of - moved).at[2:2 + 2 * pairs:2].set(sink + moved)
    return tallies[jax.random.permutation(jax.random.fold_in(stream_key, 2), count)]


def bell_draw(stream_key, dims, scale, limit, shards=(), kind=jnp.bfloat16):
    factor_of = shard_levels(stream_key, dims, shards, -0.22, 0.18) if shards else 1.0
    values = jax.random.normal(stream_key, dims, jnp.float32) * scale * factor_of
    return jnp.minimum(jnp.maximum(values, -limit), limit).astype(kind)


def bell_draw_with(rng, shape, deviation, most, pieces, heavy, dtype=jnp.bfloat16):
    drawn = deviation * jax.random.normal(rng, shape, jnp.float32)
    if pieces:
        drawn = drawn * shard_levels(rng, shape, pieces, -0.22, 0.18)
    return jnp.clip(strengthened(drawn, jax.random.fold_in(rng, 3), *heavy), -most, most).astype(dtype)


def setup_inputs(seed: int = 0) -> dict:
    key_of = jax.random.split(jax.random.key(seed), 7)
    return {
        "query": draw_query(jax.random.fold_in(key_of[6], 71), 0),
        "keys": draw_keys(jax.random.fold_in(key_of[6], 71), 0),
        "values": bell_draw(key_of[2], (TOKENS, H * HEAD_DIM), 1.0, 6.0, ((0, 64), (1, 8))),
        "shot_ids": jnp.searchsorted(jnp.cumsum(uneven(key_of[3], SHOTS, TOKENS, SHOT_MOST, 2)), jnp.arange(TOKENS), side="right").astype(jnp.int32),
        "routes": draw_routes(jax.random.fold_in(key_of[6], 71), 0),
        "out_weight": bell_draw_with(key_of[5], (H * HEAD_DIM, H * HEAD_DIM), (H * HEAD_DIM) ** -0.5, 0.15625, ((0, 8),), (0, 1, 8, 2.0)),
    }


NEGATIVE = -1e30


def rounded(array):
    return lax.optimization_barrier(array.astype(jnp.bfloat16)).astype(jnp.float32)


def reference(query, keys, values, shot_ids, routes, out_weight):
    tokens, width = query.shape
    heads = width // HEAD_DIM
    scale = HEAD_DIM ** -0.5
    block_rows = 256
    per_block = block_rows // STRETCH
    margin = SHOT_MOST
    span = block_rows + 2 * margin
    padded_keys = jnp.pad(keys, ((margin, margin), (0, 0)))
    padded_values = jnp.pad(values, ((margin, margin), (0, 0)))
    padded_ids = jnp.pad(shot_ids, (margin, margin), constant_values=-1)
    key_stretches = keys.reshape(STRETCHES, STRETCH, width)
    value_stretches = values.reshape(STRETCHES, STRETCH, width)

    def block(index):
        start = (index * block_rows).astype(jnp.int32)
        queries = lax.dynamic_slice_in_dim(query, start, block_rows, 0).astype(jnp.float32).reshape(block_rows, heads, HEAD_DIM)
        near_keys = lax.dynamic_slice_in_dim(padded_keys, start, span, 0).astype(jnp.float32).reshape(span, heads, HEAD_DIM)
        near_values = lax.dynamic_slice_in_dim(padded_values, start, span, 0).astype(jnp.float32).reshape(span, heads, HEAD_DIM)
        query_ids = lax.dynamic_slice_in_dim(shot_ids, start, block_rows, 0)
        near_ids = lax.dynamic_slice_in_dim(padded_ids, start, span, 0)
        same = query_ids[:, None] == near_ids[None, :]
        shot_scores = jnp.einsum("qhd,khd->hqk", queries, near_keys) * scale
        shot_scores = jnp.where(same[None], shot_scores, NEGATIVE)
        shot_top = jnp.max(shot_scores, axis=2)
        shot_weights = jnp.exp(shot_scores - shot_top[:, :, None])
        shot_mass = jnp.sum(shot_weights, axis=2)
        shot_sum = jnp.einsum("hqk,khd->hqd", rounded(shot_weights), near_values)
        chosen = lax.dynamic_slice_in_dim(routes, (index * per_block).astype(jnp.int32), per_block, 0)
        routed_keys = key_stretches[chosen].astype(jnp.float32).reshape(per_block, K, STRETCH, heads, HEAD_DIM)
        routed_values = value_stretches[chosen].astype(jnp.float32).reshape(per_block, K, STRETCH, heads, HEAD_DIM)
        grouped = queries.reshape(per_block, STRETCH, heads, HEAD_DIM)
        routed_scores = jnp.einsum("cqhd,cjkhd->hcqjk", grouped, routed_keys) * scale
        routed_top = jnp.max(routed_scores, axis=4)
        routed_weights = jnp.exp(routed_scores - routed_top[..., None])
        routed_mass = jnp.sum(routed_weights, axis=4)
        routed_sum = jnp.einsum("hcqjk,cjkhd->hcqjd", rounded(routed_weights), routed_values)
        routed_mean = rounded(routed_sum / routed_mass[..., None])
        shot_top = shot_top.reshape(heads, per_block, STRETCH)
        overall = jnp.maximum(shot_top, jnp.max(routed_top, axis=3))
        shot_factor = jnp.exp(shot_top - overall)
        routed_factor = jnp.exp(routed_top - overall[..., None])
        total = shot_factor * shot_mass.reshape(heads, per_block, STRETCH) + jnp.sum(routed_factor * routed_mass, axis=3)
        summed = shot_factor[..., None] * shot_sum.reshape(heads, per_block, STRETCH, HEAD_DIM)
        summed = summed + jnp.sum((routed_factor * routed_mass)[..., None] * routed_mean, axis=3)
        result = summed / total[..., None]
        return jnp.transpose(result, (1, 2, 0, 3)).reshape(block_rows, width).astype(jnp.bfloat16)

    attended = lax.map(block, jnp.arange(tokens // block_rows)).reshape(tokens, width)
    group = width // GROUPS

    def project(group_index, total):
        start = (group_index * group).astype(jnp.int32)
        columns = lax.dynamic_slice_in_dim(attended, start, group, 1)
        rows = lax.dynamic_slice_in_dim(out_weight, start, group, 0)
        return total + rounded(jnp.dot(columns, rows, preferred_element_type=jnp.float32))

    mixed = lax.fori_loop(0, GROUPS, project, jnp.zeros((tokens, width), jnp.float32))
    return mixed.astype(jnp.bfloat16)
```

```python
import functools
import math

import jax
import jax.numpy as jnp
from jax import lax
from jax.experimental import pallas as pl
from jax.experimental.pallas import tpu as pltpu
from jax.sharding import PartitionSpec as P

D = 128
ROWS = 256
STRETCH = 64
ROUTES = 8
SEQ = 64
PER = ROWS // STRETCH
NY = 8
COLS = 6
TOKENS = SEQ * ROWS
HALF = 4 * ROWS
SUB = 128
REACH = 1024
WINDOW = SUB + 2 * REACH
NEGATIVE = -1e30
FACTOR = D ** -0.5 * math.log2(math.e)
NT = (((1,), (1,)), ((), ()))
RIGHT, LEFT = 0, 1


def kernel(q_ref, k_ref, v_ref, ids_ref, routes_ref, w_ref, out_ref,
           kbuf, vbuf, qbuf, att, gbuf, wbuf, top_s, mass_s, acc_s,
           qs, qr, ring_s, ring_r, sib_s, sib_r, w_s, w_r, back_s, back_r,
           xs, xr, x2s, x2r, xsib_s, xsib_r):
    p = lax.axis_index("seq")
    hd = lax.axis_index("head")
    z, y = p // NY, p % NY
    x, c = hd // 2, hd % 2
    sibling = (p, 2 * x + 1 - c)
    bufs = (kbuf, vbuf)

    def remote(src, dst, send, recv, device):
        return pltpu.make_async_remote_copy(
            src_ref=src, dst_ref=dst, send_sem=send, recv_sem=recv,
            device_id=device, device_id_type=pl.DeviceIdType.MESH)

    def arrived(ref, sem):
        pltpu.make_async_copy(ref, ref, sem).wait()

    def sent(ref, sem):
        pltpu.make_async_copy(ref, ref, sem).wait()

    barrier = pltpu.get_barrier_semaphore()
    peers = [sibling]
    for d in range(1, NY):
        there = z * NY + (y + d) % NY
        peers += [(there, hd), (there, 2 * x + 1 - c)]
    zr, zl = (z + 1) % 8 * NY + y, (z + 7) % 8 * NY + y
    peers += [(zr, hd), (zl, hd)]
    for d in range(1, 4):
        xo = (x + d) % 4
        peers += [(p, 2 * xo), (p, 2 * xo + 1)]
    for device in peers:
        pl.semaphore_signal(barrier, inc=1, device_id=device,
                            device_id_type=pl.DeviceIdType.MESH)
    pl.semaphore_wait(barrier, len(peers))

    core = y // 4
    row0, q0 = p * PER, y % 4 * PER
    for t, (src, dst, at) in enumerate(((k_ref, kbuf, row0), (v_ref, vbuf, row0), (q_ref, qbuf, q0))):
        for i in range(3):
            h = 3 * c + i
            part = src.at[:, :, i * D:(i + 1) * D]
            own = jnp.logical_and(h == y, core == c)

            @pl.when(jnp.logical_not(own))
            def _():
                remote(part, dst.at[pl.ds(at, PER)], qs.at[i, t], qr.at[y % 4, t],
                       (z * NY + h, 2 * x + core)).start()

            @pl.when(own)
            def _():
                pltpu.make_async_copy(part, dst.at[pl.ds(at, PER)], qr.at[y % 4, t]).start()

    w_here = wbuf.at[pl.ds(pl.multiple_of(hd * 384, 384), 384)]
    for d in range(1, 8):
        other = (hd + d) % 8
        remote(w_ref.at[:, pl.ds(pl.multiple_of(other * 384, 384), 384)], w_here,
               w_s.at[d], w_r.at[d], (p, other)).start()
    w_own = pltpu.make_async_copy(
        w_ref.at[:, pl.ds(pl.multiple_of(hd * 384, 384), 384)], w_here, w_s.at[0])
    w_own.start()

    def half(t, row, core_of):
        return bufs[t].at[pl.ds((row * 2 + core_of) * (HALF // STRETCH), HALF // STRETCH)]

    def to_sibling(t, o, row):
        ref = half(t, row, c)
        return remote(ref, ref, sib_s.at[o, t], sib_r.at[o, t], sibling)

    def hop(t, way, step, row):
        ref = half(t, row, c)
        return remote(ref, ref, ring_s.at[way, step, t], ring_r.at[way, step, t],
                      (zr if way == RIGHT else zl, hd))

    def origin(way, step):
        return (z + 8 - 1 - step) % 8 if way == RIGHT else (z + 1 + step) % 8

    def slot(way, step):
        return 1 + 2 * step + way if step < 3 else 7

    def goes(t, way, step):
        return step < 3 or t == way

    def shot(b):
        start = (z * 2 + c) * (HALF // SUB) + b
        pieces = [(start + n + TOKENS // SUB - REACH // SUB) % (TOKENS // SUB)
                  for n in range(WINDOW // SUB)]
        rows = [pl.ds(n * (SUB // STRETCH), SUB // STRETCH) for n in pieces]
        at = pl.ds(pl.multiple_of(b * SUB, SUB), SUB)
        q = qbuf[pl.ds(b * (SUB // STRETCH), SUB // STRETCH)].reshape(SUB, D)
        mine = jnp.broadcast_to(ids_ref[pl.ds(start, 1), :], (SUB, SUB)).T
        scores = []
        peak = None
        for n, r in zip(pieces, rows):
            s = lax.dot_general(q, kbuf[r].reshape(SUB, D), NT, preferred_element_type=jnp.float32)
            s = jnp.where(mine == ids_ref[pl.ds(n, 1), :], s, NEGATIVE)
            peak = s if peak is None else jnp.maximum(peak, s)
            scores.append(s)
        top = jnp.max(peak, axis=1, keepdims=True)
        total = None
        acc = None
        for s, r in zip(scores, rows):
            e = jnp.exp2((s - top) * FACTOR)
            total = e if total is None else total + e
            one = jnp.dot(e.astype(jnp.bfloat16), vbuf[r].reshape(SUB, D), preferred_element_type=jnp.float32)
            acc = one if acc is None else acc + one
        mass = jnp.sum(total, axis=1, keepdims=True)
        top_s[at, :] = jnp.broadcast_to(top, (SUB, D))
        mass_s[at, :] = jnp.broadcast_to(mass, (SUB, D))
        acc_s[at, :] = acc

    def routed(b, g):
        at = pl.ds(pl.multiple_of(b * ROWS + g * STRETCH, STRETCH), STRETCH)
        stretch = (z * 2 + c) * 16 + b * 4 + g
        rows = [routes_ref[j, stretch] for j in range(ROUTES)]
        keys = jnp.concatenate([kbuf[r] for r in rows], axis=0)
        s = lax.dot_general(qbuf[b * PER + g], keys, NT, preferred_element_type=jnp.float32)
        before = top_s[at, :]
        top = jnp.maximum(before, jnp.max(s, axis=1, keepdims=True))
        e = jnp.exp2((s - top[:, :1]) * FACTOR)
        keep = jnp.exp2((before - top) * FACTOR)
        mass = keep * mass_s[at, :] + jnp.sum(e, axis=1, keepdims=True)
        vals = jnp.concatenate([vbuf[r] for r in rows], axis=0)
        summed = keep * acc_s[at, :] + jnp.dot(e.astype(jnp.bfloat16), vals,
                                               preferred_element_type=jnp.float32)
        att[b, pl.ds(pl.multiple_of(g * STRETCH, STRETCH), STRETCH), :] = (
            summed / mass).astype(jnp.bfloat16)

    def back(b):
        to = 4 * c + b
        piece = gbuf.at[6 * x + y]
        device = (z * NY + to, 2 * x + y // 3)
        own = jnp.logical_and(to == y, y // 3 == c)
        return piece, device, own

    @pl.when(y < COLS)
    def _():
        for t in range(2):
            for n in range(4):
                arrived(kbuf.at[pl.ds(0, PER)], qr.at[n, t])
            hop(t, RIGHT, 0, z).start()
            hop(t, LEFT, 0, z).start()
            to_sibling(t, 0, z).start()
        for n in range(4):
            arrived(qbuf.at[pl.ds(0, PER)], qr.at[n, 2])

        def pass_on(step):
            for t in range(2):
                for way in (RIGHT, LEFT):
                    if not goes(t, way, step):
                        continue
                    row = origin(way, step)
                    arrived(half(t, row, c), ring_r.at[way, step, t])
                    if step < 3 and goes(t, way, step + 1):
                        hop(t, way, step + 1, row).start()
                    to_sibling(t, slot(way, step), row).start()

        def from_sibling(o, row):
            for t in range(2):
                arrived(half(t, row, 1 - c), sib_r.at[o, t])

        def shots(first, last):
            pl.loop(first, last)(shot)

        pass_on(0)
        from_sibling(0, z)
        from_sibling(slot(RIGHT, 0), origin(RIGHT, 0))
        from_sibling(slot(LEFT, 0), origin(LEFT, 0))
        shots(0, 3)
        pass_on(1)
        shots(3, 6)
        pass_on(2)
        shots(6, 8)
        pass_on(3)
        for step in (1, 2):
            for way in (RIGHT, LEFT):
                from_sibling(slot(way, step), origin(way, step))
        from_sibling(7, origin(RIGHT, 3))

        for b in range(4):
            pl.loop(0, 4)(functools.partial(routed, b))
            piece, device, own = back(b)

            @pl.when(jnp.logical_not(own))
            def _():
                remote(att.at[b], piece, back_s.at[b], back_r.at[y % 3], device).start()

            @pl.when(own)
            def _():
                pltpu.make_async_copy(att.at[b], piece, back_r.at[y % 3]).start()

    xright, xleft = (p, (x + 1) % 4 * 2 + c), (p, (x + 3) % 4 * 2 + c)
    beside = (xright, xleft)
    top_rows, low_rows = pl.ds(0, ROWS // 2), pl.ds(ROWS // 2, ROWS // 2)
    parts = (top_rows, low_rows)
    sends = []

    def go(copy):
        copy.start()
        sends.append(copy)

    for i in range(3):
        ref = gbuf.at[3 * hd + i]
        arrived(ref, back_r.at[i])
        for way in (RIGHT, LEFT):
            go(remote(ref, ref, xs.at[way, i], xr.at[way, i], beside[way]))
        go(remote(ref, ref, xsib_s.at[0, i], xsib_r.at[0, i], sibling))
    for i in range(3):
        for way in (RIGHT, LEFT):
            xo = (x + 3) % 4 if way == RIGHT else (x + 1) % 4
            ref = gbuf.at[3 * (2 * xo + c) + i]
            arrived(ref, xr.at[way, i])
            cut = gbuf.at[3 * (2 * xo + c) + i, parts[way]]
            go(remote(cut, cut, x2s.at[way, i], x2r.at[way, i], beside[way]))
            go(remote(ref, ref, xsib_s.at[1 + way, i], xsib_r.at[1 + way, i], sibling))
    far = (x + 2) % 4
    for i in range(3):
        for way in (RIGHT, LEFT):
            cut = gbuf.at[3 * (2 * far + c) + i, parts[way]]
            arrived(cut, x2r.at[way, i])
            go(remote(cut, cut, xsib_s.at[3 + way, i], xsib_r.at[3 + way, i], sibling))
    for i in range(3):
        for o, xo in ((0, x), (1, (x + 3) % 4), (2, (x + 1) % 4)):
            arrived(gbuf.at[3 * (2 * xo + 1 - c) + i], xsib_r.at[o, i])
        for way in (RIGHT, LEFT):
            arrived(gbuf.at[3 * (2 * far + 1 - c) + i, parts[way]], xsib_r.at[3 + way, i])
    w_own.wait()
    for d in range(1, 8):
        arrived(w_here, w_r.at[d])

    left = jnp.concatenate([gbuf[n] for n in range(24)], axis=1)
    out_ref[...] = jnp.dot(left, wbuf[...], preferred_element_type=jnp.float32).astype(jnp.bfloat16)

    for copy in sends:
        copy.wait_send()
    for d in range(1, 8):
        sent(w_here, w_s.at[d])
    for t in range(3):
        for i in range(3):
            own = jnp.logical_and(3 * c + i == y, core == c)

            @pl.when(jnp.logical_not(own))
            def _():
                sent(qbuf.at[pl.ds(0, PER)], qs.at[i, t])

    @pl.when(y < COLS)
    def _():
        for t in range(2):
            to_sibling(t, 0, z).wait_send()
            for step in range(4):
                for way in (RIGHT, LEFT):
                    if goes(t, way, step):
                        hop(t, way, step, z).wait_send()
                        to_sibling(t, slot(way, step), z).wait_send()
        for b in range(4):
            piece, device, own = back(b)

            @pl.when(jnp.logical_not(own))
            def _():
                sent(att.at[b], back_s.at[b])


def shards(query, keys, values, shot_ids, routes, out_weight):
    vmem, hbm = pl.BlockSpec(memory_space=pltpu.VMEM), pl.BlockSpec(memory_space=pl.ANY)
    dma = pltpu.SemaphoreType.DMA
    return pl.pallas_call(
        kernel,
        out_shape=jax.ShapeDtypeStruct((ROWS, 384), jnp.bfloat16),
        in_specs=[hbm, hbm, hbm, vmem, pl.BlockSpec(memory_space=pltpu.SMEM), hbm],
        out_specs=vmem,
        scratch_shapes=[
            pltpu.VMEM((TOKENS // STRETCH, STRETCH, D), jnp.bfloat16),
            pltpu.VMEM((TOKENS // STRETCH, STRETCH, D), jnp.bfloat16),
            pltpu.VMEM((HALF // STRETCH, STRETCH, D), jnp.bfloat16),
            pltpu.VMEM((4, ROWS, D), jnp.bfloat16),
            pltpu.VMEM((24, ROWS, D), jnp.bfloat16),
            pltpu.VMEM((3072, 384), jnp.bfloat16),
            pltpu.VMEM((HALF, D), jnp.float32),
            pltpu.VMEM((HALF, D), jnp.float32),
            pltpu.VMEM((HALF, D), jnp.float32),
            dma((3, 3)), dma((4, 3)),
            dma((2, 4, 2)), dma((2, 4, 2)),
            dma((8, 2)), dma((8, 2)),
            dma((8,)), dma((8,)),
            dma((4,)), dma((3,)),
            dma((2, 3)), dma((2, 3)),
            dma((2, 3)), dma((2, 3)),
            dma((5, 3)), dma((5, 3)),
        ],
        compiler_params=pltpu.CompilerParams(
            collective_id=0, has_side_effects=True, vmem_limit_bytes=48 * 1024 * 1024),
        cost_estimate=pl.CostEstimate(
            flops=2_400_000_000, bytes_accessed=4_000_000, transcendentals=3_000_000),
    )(*(a.reshape(PER, STRETCH, 384) for a in (query, keys, values)), shot_ids.reshape(TOKENS // SUB, SUB), routes.T, out_weight)


def solution(mesh):
    placed = (P("seq", "head"), P("seq", "head"), P("seq", "head"), P(), P(), P("head", None))
    return jax.shard_map(
        shards, mesh=mesh, in_specs=placed, out_specs=P("seq", "head"), check_vma=False
    )
```

```python
import math

import jax
import jax.numpy as jnp
from jax import lax
from jax.experimental import pallas as pl
from jax.experimental.pallas import tpu as pltpu
from jax.sharding import PartitionSpec as P

D = 128
ROWS = 256
STRETCH = 64
ROUTES = 8
SEQ = 64
PER = ROWS // STRETCH
NY = 8
SPARE = 3
TOKENS = SEQ * ROWS
HALF = 4 * ROWS
SUB = 128
REACH = 1024
WINDOW = SUB + 2 * REACH
NEGATIVE = -1e30
FACTOR = D ** -0.5 * math.log2(math.e)
NT = (((1,), (1,)), ((), ()))
RIGHT, LEFT = 0, 1


def kernel(q_ref, k_ref, v_ref, ids_hbm, routes_hbm, w_ref, out_ref,
           ids_ref, routes_ref, small, kv, qbuf, att, gbuf, wbuf, total, top_s, mass_s, acc_s,
           qs, qr, ring_s, ring_r, sib_s, sib_r, hand_s, hand_r, spare_s, w_s, w_r, back_s, back_r,
           xs, xr, x2s, x2r, xsib_s, xsib_r):
    p = lax.axis_index("seq")
    hd = lax.axis_index("head")
    z, y = p // NY, p % NY
    x, c = hd // 2, hd % 2
    sibling = (p, 2 * x + 1 - c)

    def remote(src, dst, send, recv, device):
        return pltpu.make_async_remote_copy(
            src_ref=src, dst_ref=dst, send_sem=send, recv_sem=recv,
            device_id=device, device_id_type=pl.DeviceIdType.MESH)

    def arrived(ref, sem):
        pltpu.make_async_copy(ref, ref, sem).wait()

    def sent(ref, sem):
        pltpu.make_async_copy(ref, ref, sem).wait()

    ids_copy = pltpu.make_async_copy(ids_hbm, ids_ref, small.at[0])
    routes_copy = pltpu.make_async_copy(routes_hbm, routes_ref, small.at[1])
    ids_copy.start()
    routes_copy.start()

    barrier = pltpu.get_barrier_semaphore()
    peers = [sibling]
    for d in range(1, NY):
        there = z * NY + (y + d) % NY
        peers += [(there, hd), (there, 2 * x + 1 - c)]
    zr, zl = (z + 1) % 8 * NY + y, (z + 7) % 8 * NY + y
    peers += [(zr, hd), (zl, hd)]
    for d in range(1, 4):
        xo = (x + d) % 4
        peers += [(p, 2 * xo), (p, 2 * xo + 1)]
    for device in peers:
        pl.semaphore_signal(barrier, inc=1, device_id=device,
                            device_id_type=pl.DeviceIdType.MESH)
    pl.semaphore_wait(barrier, len(peers))

    core = y // 4
    row0, q0 = p * PER, y % 4 * PER
    own_k = kv.at[pl.ds(row0, PER), :, 0:D]
    own_v = kv.at[pl.ds(row0, PER), :, D:2 * D]
    own_q = qbuf.at[pl.ds(q0, PER)]
    turned = (y + 10 - 4 * c) % 8 // 4

    def to_column(n, t, src, dst):
        i = n + turned * (2 - 2 * n)
        h = 4 * c + i
        own = h == y
        part = src.at[:, :, pl.ds(pl.multiple_of(i * D, D), D)]

        @pl.when(jnp.logical_not(own))
        def _():
            remote(part, dst, qs.at[n, t], qr.at[y % 4, t], (z * NY + h, 2 * x + core)).start()

        @pl.when(own)
        def _():
            pltpu.make_async_copy(part, dst, qr.at[y % 4, t]).start()

    def left_for_column(n, t):
        h = 4 * c + n + turned * (2 - 2 * n)

        @pl.when(h != y)
        def _():
            sent(qbuf.at[pl.ds(0, PER)], qs.at[n, t])

    def queries_to_columns():
        for n in range(3):
            to_column(n, 2, q_ref, own_q)

    for n in range(3):
        to_column(n, 0, k_ref, own_k)
        to_column(n, 1, v_ref, own_v)

    w_here = wbuf.at[pl.ds(3 * hd, 3)]

    def w_part(of):
        return w_ref.at[:, :, pl.ds(pl.multiple_of(of * 384, 384), 384)]

    for d in range(1, 8):
        other = (hd + d) % 8
        remote(w_part(other), w_here, w_s.at[d], w_r.at[d], (p, other)).start()
    w_own = pltpu.make_async_copy(w_part(hd), w_here, w_s.at[0])
    w_own.start()

    def nth(k, core_of):
        return (y + 2 * ((y // 4 + core_of) % 2) + (0, 1, 3, 2)[k]) % 4

    def piece_of(row, core_of, n):
        return kv.at[pl.ds((row * NY + 4 * core_of + n) * PER, PER)]

    def half_of(row, core_of):
        return kv.at[pl.ds((row * NY + 4 * core_of) * PER, 4 * PER)]

    def to_sibling(o, row, n):
        ref = piece_of(row, c, n)
        return remote(ref, ref, sib_s.at[o], sib_r.at[o], sibling)

    def hop(way, step, ref, n):
        return remote(ref, ref, ring_s.at[way, step, n], ring_r.at[way, step, n],
                      (zr if way == RIGHT else zl, hd))

    lean = jnp.logical_xor(core == c, y % 4 == 0)

    def in_ring(n):
        return jnp.logical_not(jnp.logical_and(lean, n == SPARE))

    def origin(way, step):
        return (z + 8 - 1 - step) % 8 if way == RIGHT else (z + 1 + step) % 8

    def slot(way, step):
        return 1 + 2 * step + way if step < 3 else 7

    def goes(k, way, step):
        return step < 3 or k // 2 == way

    def shot(b):
        start = (z * 2 + c) * (HALF // SUB) + b
        pieces = [(start + n + TOKENS // SUB - REACH // SUB) % (TOKENS // SUB)
                  for n in range(WINDOW // SUB)]
        rows = [pl.ds(n * (SUB // STRETCH), SUB // STRETCH) for n in pieces]
        at = pl.ds(pl.multiple_of(b * SUB, SUB), SUB)
        q = qbuf[pl.ds(b * (SUB // STRETCH), SUB // STRETCH)].reshape(SUB, D)
        mine = jnp.broadcast_to(ids_ref[pl.ds(start, 1), :], (SUB, SUB)).T
        scores = []
        peak = None
        for n, r in zip(pieces, rows):
            s = lax.dot_general(q, kv[r, :, 0:D].reshape(SUB, D), NT, preferred_element_type=jnp.float32)
            s = jnp.where(mine == ids_ref[pl.ds(n, 1), :], s, NEGATIVE)
            peak = s if peak is None else jnp.maximum(peak, s)
            scores.append(s)
        top = jnp.max(peak, axis=1, keepdims=True)
        added = None
        acc = None
        for s, r in zip(scores, rows):
            e = jnp.exp2((s - top) * FACTOR)
            added = e if added is None else added + e
            one = jnp.dot(e.astype(jnp.bfloat16), kv[r, :, D:2 * D].reshape(SUB, D), preferred_element_type=jnp.float32)
            acc = one if acc is None else acc + one
        mass = jnp.sum(added, axis=1, keepdims=True)
        top_s[at, :] = jnp.broadcast_to(top, (SUB, D))
        mass_s[at, :] = jnp.broadcast_to(mass, (SUB, D))
        acc_s[at, :] = acc

    def routed(b):
        ats = [pl.ds(pl.multiple_of(b * ROWS, ROWS) + g * STRETCH, STRETCH) for g in range(PER)]
        stretch = (z * 2 + c) * 16 + b * PER
        rows = [[routes_ref[j, stretch + g] for j in range(ROUTES)] for g in range(PER)]
        scores = []
        for g in range(PER):
            keys = jnp.concatenate([kv[r, :, 0:D] for r in rows[g]], axis=0)
            scores.append(lax.dot_general(qbuf[b * PER + g], keys, NT,
                                          preferred_element_type=jnp.float32))
        before = [top_s[at, :] for at in ats]
        tops = [jnp.maximum(t, jnp.max(s, axis=1, keepdims=True)) for t, s in zip(before, scores)]
        exps = [jnp.exp2((s - t[:, :1]) * FACTOR) for s, t in zip(scores, tops)]
        keeps = [jnp.exp2((o - t) * FACTOR) for o, t in zip(before, tops)]
        sums = []
        for g in range(PER):
            vals = jnp.concatenate([kv[r, :, D:2 * D] for r in rows[g]], axis=0)
            sums.append(jnp.dot(exps[g].astype(jnp.bfloat16), vals,
                                preferred_element_type=jnp.float32))
        for g in range(PER):
            mass = keeps[g] * mass_s[ats[g], :] + jnp.sum(exps[g], axis=1, keepdims=True)
            summed = keeps[g] * acc_s[ats[g], :] + sums[g]
            att[b, g * STRETCH:(g + 1) * STRETCH, :] = (summed / mass).astype(jnp.bfloat16)

    def back(b):
        to = 4 * c + b
        return gbuf.at[6 * x + 3 * core + y % 4], (z * NY + to, 2 * x + core), to == y

    ids_copy.wait()
    routes_copy.wait()

    @pl.when(y % 4 < SPARE)
    def _():
        def own(k):
            n = nth(k, c)
            ref = piece_of(z, c, n)
            for t in range(2):
                arrived(qbuf.at[pl.ds(0, PER)], qr.at[n, t])

            @pl.when(in_ring(n))
            def _():
                hop(RIGHT, 0, ref, n).start()
                hop(LEFT, 0, ref, n).start()

            to_sibling(0, z, n).start()

        def pass_on(step, k):
            n = nth(k, c)

            @pl.when(in_ring(n))
            def _():
                for way in (RIGHT, LEFT):
                    if goes(k, way, step):
                        row = origin(way, step)
                        ref = piece_of(row, c, n)
                        arrived(ref, ring_r.at[way, step, n])
                        if step < 3 and goes(k, way, step + 1):
                            hop(way, step + 1, ref, n).start()
                        to_sibling(slot(way, step), row, n).start()

        def handed(step):
            @pl.when(lean)
            def _():
                for way in (RIGHT, LEFT)[:2 if step < 3 else 1]:
                    row = origin(way, step)
                    arrived(piece_of(row, c, SPARE), hand_r.at[slot(way, step)])
                    to_sibling(slot(way, step), row, SPARE).start()

        def from_sibling(o, row):
            arrived(half_of(row, 1 - c), sib_r.at[o])

        own(0)
        own(1)
        pass_on(0, 0)
        own(2)
        pass_on(0, 1)
        own(3)
        queries_to_columns()
        pass_on(0, 2)
        pass_on(0, 3)
        handed(0)
        for n in range(4):
            arrived(qbuf.at[pl.ds(0, PER)], qr.at[n, 2])
        from_sibling(0, z)
        from_sibling(slot(RIGHT, 0), origin(RIGHT, 0))
        from_sibling(slot(LEFT, 0), origin(LEFT, 0))
        for k in range(4):
            pl.loop(2 * k, 2 * k + 2)(shot)
            pass_on(1, k)
        handed(1)
        for step in (2, 3):
            for k in range(4):
                pass_on(step, k)
            handed(step)
        for step in (1, 2):
            for way in (RIGHT, LEFT):
                from_sibling(slot(way, step), origin(way, step))
        from_sibling(7, origin(RIGHT, 3))

        for k in range(4):
            b = (k + y) % 4
            routed(b)
            piece, device, mine = back(b)

            @pl.when(jnp.logical_not(mine))
            def _():
                remote(att.at[b], piece, back_s.at[k], back_r.at[y % 4], device).start()

            @pl.when(mine)
            def _():
                pltpu.make_async_copy(att.at[b], piece, back_r.at[y % 4]).start()

    paired = jnp.where(core == c, 1, 0)

    def served(j):
        return paired * (2 - j), (y + 9 - paired * (2 + j)) % NY

    def each(fn):
        fn(0)

        @pl.when(paired == 1)
        def _():
            fn(1)

    def spare_piece(row, j):
        return kv.at[pl.ds((row * NY + j) * PER, PER)]

    def spare_goes(j, way, step):
        return step < 3 or j == way

    def hand(o, row, j):
        return remote(spare_piece(row, j), kv.at[pl.ds((row * NY + y) * PER, PER)],
                      hand_s.at[o, j], hand_r.at[o],
                      (z * NY + served(j)[1], 2 * x + core))

    @pl.when(y % 4 == SPARE)
    def _():
        def fetch(j):
            lanes = pl.ds(pl.multiple_of(served(j)[0] * D, D), D)
            at = pl.ds((z * NY + j) * PER, PER)
            return [pltpu.make_async_copy(src.at[:, :, lanes], kv.at[at, :, t * D:(t + 1) * D],
                                          spare_s.at[j, t]) for t, src in enumerate((k_ref, v_ref))]

        def begin(j):
            for copy in fetch(j):
                copy.start()

        def launch(j):
            for copy in fetch(j):
                copy.wait()
            for way in (RIGHT, LEFT):
                hop(way, 0, spare_piece(z, j), j).start()

        each(begin)
        each(launch)
        for step in range(4):
            def carry(j):
                for way in (RIGHT, LEFT):
                    if spare_goes(j, way, step):
                        row = origin(way, step)
                        arrived(spare_piece(row, j), ring_r.at[way, step, j])
                        if step < 3 and spare_goes(j, way, step + 1):
                            hop(way, step + 1, spare_piece(row, j), j).start()
                        hand(slot(way, step), row, j).start()

            each(carry)
            if step == 0:
                for n in range(3):
                    left_for_column(n, 0)
                    left_for_column(n, 1)
                queries_to_columns()

    xright, xleft = (p, (x + 1) % 4 * 2 + c), (p, (x + 3) % 4 * 2 + c)
    beside = (xright, xleft)
    parts = (pl.ds(0, ROWS // 2), pl.ds(ROWS // 2, ROWS // 2))
    far = (x + 2) % 4
    came = ((x + 3) % 4, (x + 1) % 4)

    def from_columns(i):
        ref = gbuf.at[3 * hd + i]
        arrived(ref, back_r.at[i])
        for way in (RIGHT, LEFT):
            remote(ref, ref, xs.at[way, i], xr.at[way, i], beside[way]).start()
        remote(ref, ref, xsib_s.at[0, i], xsib_r.at[0, i], sibling).start()

    def from_beside(i):
        for way in (RIGHT, LEFT):
            at = 3 * (2 * came[way] + c) + i
            ref, cut = gbuf.at[at], gbuf.at[at, parts[way]]
            arrived(ref, xr.at[way, i])
            remote(cut, cut, x2s.at[way, i], x2r.at[way, i], beside[way]).start()
            remote(ref, ref, xsib_s.at[1 + way, i], xsib_r.at[1 + way, i], sibling).start()

    def from_far(i):
        for way in (RIGHT, LEFT):
            cut = gbuf.at[3 * (2 * far + c) + i, parts[way]]
            arrived(cut, x2r.at[way, i])
            remote(cut, cut, xsib_s.at[3 + way, i], xsib_r.at[3 + way, i], sibling).start()

    def project(core_of, i):
        left = jnp.concatenate([gbuf[3 * (2 * n + core_of) + i] for n in range(4)], axis=1)
        right = jnp.concatenate([wbuf[3 * (2 * n + core_of) + i] for n in range(4)], axis=0)
        total[...] += jnp.dot(left, right, preferred_element_type=jnp.float32)

    def project_own(i):
        project(c, i)

    def project_sibling(i):
        for o, xo in ((0, x), (1, came[RIGHT]), (2, came[LEFT])):
            arrived(gbuf.at[3 * (2 * xo + 1 - c) + i], xsib_r.at[o, i])
        for way in (RIGHT, LEFT):
            arrived(gbuf.at[3 * (2 * far + 1 - c) + i, parts[way]], xsib_r.at[3 + way, i])
        project(1 - c, i)

    def in_turn(n, stage):
        i = (y + 4 - n) % 4

        @pl.when(i < 3)
        def _():
            stage(i)

    total[...] = jnp.zeros((ROWS, 384), jnp.float32)
    w_own.wait()
    for d in range(1, 8):
        arrived(w_here, w_r.at[d])
    for turn in range(7):
        for late, stage in enumerate((from_columns, from_beside, from_far, project_own)):
            if 0 <= turn - late < 4:
                in_turn(turn - late, stage)
    for turn in range(4):
        in_turn(turn, project_sibling)

    out_ref[...] = total[...].astype(jnp.bfloat16)

    for i in range(3):
        for way in (RIGHT, LEFT):
            sent(gbuf.at[0], xs.at[way, i])
            sent(gbuf.at[0, parts[way]], x2s.at[way, i])
            sent(gbuf.at[0, parts[way]], xsib_s.at[3 + way, i])
        for o in range(3):
            sent(gbuf.at[0], xsib_s.at[o, i])
    for d in range(1, 8):
        sent(w_here, w_s.at[d])
    for n in range(3):
        left_for_column(n, 2)

    @pl.when(y % 4 < SPARE)
    def _():
        for n in range(3):
            left_for_column(n, 0)
            left_for_column(n, 1)
        for k in range(4):
            n = nth(k, c)
            ref = piece_of(z, c, n)

            @pl.when(in_ring(n))
            def _():
                for step in range(4):
                    for way in (RIGHT, LEFT):
                        if goes(k, way, step):
                            hop(way, step, ref, n).wait_send()

        for o in range(8):
            sent(half_of(z, c), sib_s.at[o])
        for k in range(4):
            piece, device, mine = back((k + y) % 4)

            @pl.when(jnp.logical_not(mine))
            def _():
                sent(att.at[0], back_s.at[k])

    @pl.when(y % 4 == SPARE)
    def _():
        def gone(j):
            for step in range(4):
                for way in (RIGHT, LEFT):
                    if spare_goes(j, way, step):
                        hop(way, step, spare_piece(z, j), j).wait_send()
                        hand(slot(way, step), z, j).wait_send()

        each(gone)


def shards(query, keys, values, shot_ids, routes, out_weight):
    vmem, hbm = pl.BlockSpec(memory_space=pltpu.VMEM), pl.BlockSpec(memory_space=pl.ANY)
    dma = pltpu.SemaphoreType.DMA
    return pl.pallas_call(
        kernel,
        out_shape=jax.ShapeDtypeStruct((ROWS, 384), jnp.bfloat16),
        in_specs=[hbm] * 6,
        out_specs=vmem,
        scratch_shapes=[
            pltpu.VMEM((TOKENS // SUB, SUB), jnp.int32),
            pltpu.SMEM((ROUTES, TOKENS // STRETCH), jnp.int32),
            dma((2,)),
            pltpu.VMEM((TOKENS // STRETCH, STRETCH, 2 * D), jnp.bfloat16),
            pltpu.VMEM((HALF // STRETCH, STRETCH, D), jnp.bfloat16),
            pltpu.VMEM((4, ROWS, D), jnp.bfloat16),
            pltpu.VMEM((24, ROWS, D), jnp.bfloat16),
            pltpu.VMEM((24, D, 384), jnp.bfloat16),
            pltpu.VMEM((ROWS, 384), jnp.float32),
            pltpu.VMEM((HALF, D), jnp.float32),
            pltpu.VMEM((HALF, D), jnp.float32),
            pltpu.VMEM((HALF, D), jnp.float32),
            dma((3, 3)), dma((4, 3)),
            dma((2, 4, 4)), dma((2, 4, 4)),
            dma((8,)), dma((8,)),
            dma((8, 2)), dma((8,)), dma((2, 2)),
            dma((8,)), dma((8,)),
            dma((4,)), dma((3,)),
            dma((2, 3)), dma((2, 3)),
            dma((2, 3)), dma((2, 3)),
            dma((5, 3)), dma((5, 3)),
        ],
        compiler_params=pltpu.CompilerParams(
            collective_id=0, has_side_effects=True, vmem_limit_bytes=60 * 1024 * 1024),
        cost_estimate=pl.CostEstimate(
            flops=2_400_000_000, bytes_accessed=4_000_000, transcendentals=3_000_000),
    )(*(a.reshape(PER, STRETCH, 384) for a in (query, keys, values)), shot_ids.reshape(TOKENS // SUB, SUB), routes.T, out_weight.reshape(3, D, 3072))


def solution(mesh):
    placed = (P("seq", "head"), P("seq", "head"), P("seq", "head"), P(), P(), P("head", None))
    return jax.shard_map(
        shards, mesh=mesh, in_specs=placed, out_specs=P("seq", "head"), check_vma=False
    )
```

```python
import math

import jax
import jax.numpy as jnp
from jax import lax
from jax.experimental import pallas as pl
from jax.experimental.pallas import tpu as pltpu
from jax.sharding import PartitionSpec as P

D = 128
ROWS = 256
STRETCH = 64
ROUTES = 8
SEQ = 64
PER = ROWS // STRETCH
NY = 8
SPARE = 3
TOKENS = SEQ * ROWS
HALF = 4 * ROWS
SUB = 128
REACH = 1024
WINDOW = SUB + 2 * REACH
NEGATIVE = -1e30
FACTOR = D ** -0.5 * math.log2(math.e)
NT = (((1,), (1,)), ((), ()))
RIGHT, LEFT = 0, 1


def kernel(q_ref, k_ref, v_ref, ids_hbm, routes_hbm, w_ref, out_ref,
           ids_ref, routes_ref, small, kv, qbuf, att, gbuf, wbuf, total, top_s, mass_s, acc_s,
           qs, qr, ring_s, ring_r, sib_s, sib_r, hand_s, hand_r, spare_s, w_s, w_r, back_s, back_r,
           xs, xr, x2s, x2r, xsib_s, xsib_r):
    p = lax.axis_index("seq")
    hd = lax.axis_index("head")
    z, y = p // NY, p % NY
    x, c = hd // 2, hd % 2
    sibling = (p, 2 * x + 1 - c)

    def remote(src, dst, send, recv, device):
        return pltpu.make_async_remote_copy(
            src_ref=src, dst_ref=dst, send_sem=send, recv_sem=recv,
            device_id=device, device_id_type=pl.DeviceIdType.MESH)

    def arrived(ref, sem):
        pltpu.make_async_copy(ref, ref, sem).wait()

    def sent(ref, sem):
        pltpu.make_async_copy(ref, ref, sem).wait()

    ids_copy = pltpu.make_async_copy(ids_hbm, ids_ref, small.at[0])
    routes_copy = pltpu.make_async_copy(routes_hbm, routes_ref, small.at[1])
    ids_copy.start()
    routes_copy.start()

    barrier = pltpu.get_barrier_semaphore()
    peers = [sibling]
    for d in range(1, NY):
        there = z * NY + (y + d) % NY
        peers += [(there, hd), (there, 2 * x + 1 - c)]
    zr, zl = (z + 1) % 8 * NY + y, (z + 7) % 8 * NY + y
    peers += [(zr, hd), (zl, hd)]
    for d in range(1, 4):
        xo = (x + d) % 4
        peers += [(p, 2 * xo), (p, 2 * xo + 1)]
    for device in peers:
        pl.semaphore_signal(barrier, inc=1, device_id=device,
                            device_id_type=pl.DeviceIdType.MESH)
    pl.semaphore_wait(barrier, len(peers))

    core = y // 4
    row0, q0 = p * PER, y % 4 * PER
    own_k = kv.at[pl.ds(row0, PER), :, 0:D]
    own_v = kv.at[pl.ds(row0, PER), :, D:2 * D]
    own_q = qbuf.at[pl.ds(q0, PER)]
    turned = (y + 10 - 4 * c) % 8 // 4

    def to_column(n, t, src, dst):
        i = n + turned * (2 - 2 * n)
        h = 4 * c + i
        own = h == y
        part = src.at[:, :, pl.ds(pl.multiple_of(i * D, D), D)]

        @pl.when(jnp.logical_not(own))
        def _():
            remote(part, dst, qs.at[n, t], qr.at[y % 4, t], (z * NY + h, 2 * x + core)).start()

        @pl.when(own)
        def _():
            pltpu.make_async_copy(part, dst, qr.at[y % 4, t]).start()

    def left_for_column(n, t):
        h = 4 * c + n + turned * (2 - 2 * n)

        @pl.when(h != y)
        def _():
            sent(qbuf.at[pl.ds(0, PER)], qs.at[n, t])

    def queries_to_columns():
        for n in range(3):
            to_column(n, 2, q_ref, own_q)

    for n in range(3):
        to_column(n, 0, k_ref, own_k)
        to_column(n, 1, v_ref, own_v)

    w_here = wbuf.at[pl.ds(3 * hd, 3)]

    def w_part(of):
        return w_ref.at[:, :, pl.ds(pl.multiple_of(of * 384, 384), 384)]

    for d in range(1, 8):
        other = (hd + d) % 8
        remote(w_part(other), w_here, w_s.at[d], w_r.at[d], (p, other)).start()
    w_own = pltpu.make_async_copy(w_part(hd), w_here, w_s.at[0])
    w_own.start()

    def nth(k, core_of):
        return (y + 2 * ((y // 4 + core_of) % 2) + (0, 1, 3, 2)[k]) % 4

    def piece_of(row, core_of, n, cut=(0, PER)):
        return kv.at[pl.ds((row * NY + 4 * core_of + n) * PER + cut[0], cut[1])]

    def half_of(row, core_of):
        return kv.at[pl.ds((row * NY + 4 * core_of) * PER, 4 * PER)]

    def to_sibling(o, row, n, cut=(0, PER)):
        ref = piece_of(row, c, n, cut)
        return remote(ref, ref, sib_s.at[o], sib_r.at[o], sibling)

    def hop(way, step, ref, n):
        return remote(ref, ref, ring_s.at[way, step, n], ring_r.at[way, step, n],
                      (zr if way == RIGHT else zl, hd))

    lean = jnp.logical_xor(core == c, y % 4 == 0)
    whole, lower, upper = (0, PER), (0, PER // 2), (PER // 2, PER // 2)

    def ring_part(n, fn):
        @pl.when(n != SPARE)
        def _():
            fn(whole)

        @pl.when(jnp.logical_and(n == SPARE, jnp.logical_not(lean)))
        def _():
            fn(lower)

    def origin(way, step):
        return (z + 8 - 1 - step) % 8 if way == RIGHT else (z + 1 + step) % 8

    def slot(way, step):
        return 1 + 2 * step + way if step < 3 else 7

    def goes(k, way, step):
        return step < 3 or k // 2 == way

    def shot(b):
        start = (z * 2 + c) * (HALF // SUB) + b
        pieces = [(start + n + TOKENS // SUB - REACH // SUB) % (TOKENS // SUB)
                  for n in range(WINDOW // SUB)]
        rows = [pl.ds(n * (SUB // STRETCH), SUB // STRETCH) for n in pieces]
        at = pl.ds(pl.multiple_of(b * SUB, SUB), SUB)
        q = qbuf[pl.ds(b * (SUB // STRETCH), SUB // STRETCH)].reshape(SUB, D)
        mine = jnp.broadcast_to(ids_ref[pl.ds(start, 1), :], (SUB, SUB)).T
        scores = []
        peak = None
        for n, r in zip(pieces, rows):
            s = lax.dot_general(q, kv[r, :, 0:D].reshape(SUB, D), NT, preferred_element_type=jnp.float32)
            s = jnp.where(mine == ids_ref[pl.ds(n, 1), :], s, NEGATIVE)
            peak = s if peak is None else jnp.maximum(peak, s)
            scores.append(s)
        top = jnp.max(peak, axis=1, keepdims=True)
        added = None
        acc = None
        for s, r in zip(scores, rows):
            e = jnp.exp2((s - top) * FACTOR)
            added = e if added is None else added + e
            one = jnp.dot(e.astype(jnp.bfloat16), kv[r, :, D:2 * D].reshape(SUB, D), preferred_element_type=jnp.float32)
            acc = one if acc is None else acc + one
        mass = jnp.sum(added, axis=1, keepdims=True)
        top_s[at, :] = jnp.broadcast_to(top, (SUB, D))
        mass_s[at, :] = jnp.broadcast_to(mass, (SUB, D))
        acc_s[at, :] = acc

    def routed(b):
        ats = [pl.ds(pl.multiple_of(b * ROWS, ROWS) + g * STRETCH, STRETCH) for g in range(PER)]
        stretch = (z * 2 + c) * 16 + b * PER
        rows = [[routes_ref[j, stretch + g] for j in range(ROUTES)] for g in range(PER)]
        scores = []
        for g in range(PER):
            keys = jnp.concatenate([kv[r, :, 0:D] for r in rows[g]], axis=0)
            scores.append(lax.dot_general(qbuf[b * PER + g], keys, NT,
                                          preferred_element_type=jnp.float32))
        before = [top_s[at, :] for at in ats]
        tops = [jnp.maximum(t, jnp.max(s, axis=1, keepdims=True)) for t, s in zip(before, scores)]
        exps = [jnp.exp2((s - t[:, :1]) * FACTOR) for s, t in zip(scores, tops)]
        keeps = [jnp.exp2((o - t) * FACTOR) for o, t in zip(before, tops)]
        sums = []
        for g in range(PER):
            vals = jnp.concatenate([kv[r, :, D:2 * D] for r in rows[g]], axis=0)
            sums.append(jnp.dot(exps[g].astype(jnp.bfloat16), vals,
                                preferred_element_type=jnp.float32))
        for g in range(PER):
            mass = keeps[g] * mass_s[ats[g], :] + jnp.sum(exps[g], axis=1, keepdims=True)
            summed = keeps[g] * acc_s[ats[g], :] + sums[g]
            att[b, g * STRETCH:(g + 1) * STRETCH, :] = (summed / mass).astype(jnp.bfloat16)

    def back(b):
        to = 4 * c + b
        return gbuf.at[6 * x + 3 * core + y % 4], (z * NY + to, 2 * x + core), to == y

    ids_copy.wait()
    routes_copy.wait()

    @pl.when(y % 4 < SPARE)
    def _():
        def own(k):
            n = nth(k, c)
            for t in range(2):
                arrived(qbuf.at[pl.ds(0, PER)], qr.at[n, t])

            def begin(cut):
                ref = piece_of(z, c, n, cut)
                hop(RIGHT, 0, ref, n).start()
                hop(LEFT, 0, ref, n).start()

            ring_part(n, begin)
            to_sibling(0, z, n).start()

        def pass_on(step, k):
            n = nth(k, c)

            def carry(cut):
                for way in (RIGHT, LEFT):
                    if goes(k, way, step):
                        row = origin(way, step)
                        ref = piece_of(row, c, n, cut)
                        arrived(ref, ring_r.at[way, step, n])
                        if step < 3 and goes(k, way, step + 1):
                            hop(way, step + 1, ref, n).start()
                        to_sibling(slot(way, step), row, n, cut).start()

            ring_part(n, carry)

        def handed(step):
            def take(cut):
                for way in (RIGHT, LEFT)[:2 if step < 3 else 1]:
                    row = origin(way, step)
                    arrived(piece_of(row, c, SPARE, cut), hand_r.at[slot(way, step)])
                    to_sibling(slot(way, step), row, SPARE, cut).start()

            @pl.when(lean)
            def _():
                take(whole)

            @pl.when(jnp.logical_not(lean))
            def _():
                take(upper)

        def from_sibling(o, row):
            arrived(half_of(row, 1 - c), sib_r.at[o])

        own(0)
        own(1)
        pass_on(0, 0)
        own(2)
        pass_on(0, 1)
        own(3)
        pass_on(0, 2)
        pass_on(0, 3)
        queries_to_columns()
        for k in range(4):
            pass_on(1, k)
        handed(0)
        for n in range(4):
            arrived(qbuf.at[pl.ds(0, PER)], qr.at[n, 2])
        from_sibling(0, z)
        from_sibling(slot(RIGHT, 0), origin(RIGHT, 0))
        from_sibling(slot(LEFT, 0), origin(LEFT, 0))
        for k in range(4):
            pass_on(2, k)
            pl.loop(2 * k, 2 * k + 2)(shot)
        handed(1)
        handed(2)
        for k in range(4):
            pass_on(3, k)
        handed(3)
        for step in (1, 2):
            for way in (RIGHT, LEFT):
                from_sibling(slot(way, step), origin(way, step))
        from_sibling(7, origin(RIGHT, 3))

        for k in range(4):
            b = (k + y) % 4
            routed(b)
            piece, device, mine = back(b)

            @pl.when(jnp.logical_not(mine))
            def _():
                remote(att.at[b], piece, back_s.at[k], back_r.at[y % 4], device).start()

            @pl.when(mine)
            def _():
                pltpu.make_async_copy(att.at[b], piece, back_r.at[y % 4]).start()

    def each(fn):
        for i in range(3):
            near = jnp.logical_xor(core == c, i == 0)

            @pl.when(near)
            def _():
                fn(i, whole)

            @pl.when(jnp.logical_not(near))
            def _():
                fn(i, upper)

    def spare_piece(row, i, cut):
        return kv.at[pl.ds((row * NY + i) * PER + cut[0], cut[1])]

    def spare_goes(i, way, step):
        return step < 3 or i % 2 == way

    def hand(o, row, i, cut):
        return remote(spare_piece(row, i, cut), kv.at[pl.ds((row * NY + y) * PER + cut[0], cut[1])],
                      hand_s.at[o, i], hand_r.at[o], (z * NY + 4 * c + i, 2 * x + core))

    @pl.when(y % 4 == SPARE)
    def _():
        def fetch(i, cut):
            at = spare_piece(z, i, cut)
            return [pltpu.make_async_copy(src.at[cut[0]:cut[0] + cut[1], :, i * D:(i + 1) * D],
                                          at.at[:, :, t * D:(t + 1) * D],
                                          spare_s.at[i, t]) for t, src in enumerate((k_ref, v_ref))]

        def begin(i, cut):
            for copy in fetch(i, cut):
                copy.start()

        def launch(i, cut):
            for copy in fetch(i, cut):
                copy.wait()
            for way in (RIGHT, LEFT):
                hop(way, 0, spare_piece(z, i, cut), i).start()

        each(begin)
        each(launch)
        for step in range(4):
            def carry(i, cut):
                for way in (RIGHT, LEFT):
                    if spare_goes(i, way, step):
                        row = origin(way, step)
                        ref = spare_piece(row, i, cut)
                        arrived(ref, ring_r.at[way, step, i])
                        if step < 3 and spare_goes(i, way, step + 1):
                            hop(way, step + 1, ref, i).start()
                        hand(slot(way, step), row, i, cut).start()

            each(carry)
            if step == 0:
                for n in range(3):
                    left_for_column(n, 0)
                    left_for_column(n, 1)
                queries_to_columns()

    xright, xleft = (p, (x + 1) % 4 * 2 + c), (p, (x + 3) % 4 * 2 + c)
    beside = (xright, xleft)
    parts = (pl.ds(0, ROWS // 2), pl.ds(ROWS // 2, ROWS // 2))
    far = (x + 2) % 4
    came = ((x + 3) % 4, (x + 1) % 4)

    def from_columns(i):
        ref = gbuf.at[3 * hd + i]
        arrived(ref, back_r.at[i])
        for way in (RIGHT, LEFT):
            remote(ref, ref, xs.at[way, i], xr.at[way, i], beside[way]).start()
        remote(ref, ref, xsib_s.at[0, i], xsib_r.at[0, i], sibling).start()

    def from_beside(i):
        for way in (RIGHT, LEFT):
            at = 3 * (2 * came[way] + c) + i
            ref, cut = gbuf.at[at], gbuf.at[at, parts[way]]
            arrived(ref, xr.at[way, i])
            remote(cut, cut, x2s.at[way, i], x2r.at[way, i], beside[way]).start()
            remote(ref, ref, xsib_s.at[1 + way, i], xsib_r.at[1 + way, i], sibling).start()

    def from_far(i):
        for way in (RIGHT, LEFT):
            cut = gbuf.at[3 * (2 * far + c) + i, parts[way]]
            arrived(cut, x2r.at[way, i])
            remote(cut, cut, xsib_s.at[3 + way, i], xsib_r.at[3 + way, i], sibling).start()

    def project(core_of, i):
        left = jnp.concatenate([gbuf[3 * (2 * n + core_of) + i] for n in range(4)], axis=1)
        right = jnp.concatenate([wbuf[3 * (2 * n + core_of) + i] for n in range(4)], axis=0)
        total[...] += jnp.dot(left, right, preferred_element_type=jnp.float32)

    def project_own(i):
        project(c, i)

    def project_sibling(i):
        for o, xo in ((0, x), (1, came[RIGHT]), (2, came[LEFT])):
            arrived(gbuf.at[3 * (2 * xo + 1 - c) + i], xsib_r.at[o, i])
        for way in (RIGHT, LEFT):
            arrived(gbuf.at[3 * (2 * far + 1 - c) + i, parts[way]], xsib_r.at[3 + way, i])
        project(1 - c, i)

    def in_turn(n, stage):
        i = (y + 4 - n) % 4

        @pl.when(i < 3)
        def _():
            stage(i)

    total[...] = jnp.zeros((ROWS, 384), jnp.float32)
    w_own.wait()
    for d in range(1, 8):
        arrived(w_here, w_r.at[d])
    for turn in range(7):
        for late, stage in enumerate((from_columns, from_beside, from_far, project_own)):
            if 0 <= turn - late < 4:
                in_turn(turn - late, stage)
    for turn in range(4):
        in_turn(turn, project_sibling)

    out_ref[...] = total[...].astype(jnp.bfloat16)

    for i in range(3):
        for way in (RIGHT, LEFT):
            sent(gbuf.at[0], xs.at[way, i])
            sent(gbuf.at[0, parts[way]], x2s.at[way, i])
            sent(gbuf.at[0, parts[way]], xsib_s.at[3 + way, i])
        for o in range(3):
            sent(gbuf.at[0], xsib_s.at[o, i])
    for d in range(1, 8):
        sent(w_here, w_s.at[d])
    for n in range(3):
        left_for_column(n, 2)

    @pl.when(y % 4 < SPARE)
    def _():
        for n in range(3):
            left_for_column(n, 0)
            left_for_column(n, 1)
        for k in range(4):
            n = nth(k, c)

            def gone(cut):
                for step in range(4):
                    for way in (RIGHT, LEFT):
                        if goes(k, way, step):
                            hop(way, step, piece_of(z, c, n, cut), n).wait_send()

            ring_part(n, gone)
        for o in range(8):
            sent(half_of(z, c), sib_s.at[o])
        for k in range(4):
            piece, device, mine = back((k + y) % 4)

            @pl.when(jnp.logical_not(mine))
            def _():
                sent(att.at[0], back_s.at[k])

    @pl.when(y % 4 == SPARE)
    def _():
        def gone(i, cut):
            for step in range(4):
                for way in (RIGHT, LEFT):
                    if spare_goes(i, way, step):
                        hop(way, step, spare_piece(z, i, cut), i).wait_send()
                        hand(slot(way, step), z, i, cut).wait_send()

        each(gone)


def shards(query, keys, values, shot_ids, routes, out_weight):
    vmem, hbm = pl.BlockSpec(memory_space=pltpu.VMEM), pl.BlockSpec(memory_space=pl.ANY)
    dma = pltpu.SemaphoreType.DMA
    return pl.pallas_call(
        kernel,
        out_shape=jax.ShapeDtypeStruct((ROWS, 384), jnp.bfloat16),
        in_specs=[hbm] * 6,
        out_specs=vmem,
        scratch_shapes=[
            pltpu.VMEM((TOKENS // SUB, SUB), jnp.int32),
            pltpu.SMEM((ROUTES, TOKENS // STRETCH), jnp.int32),
            dma((2,)),
            pltpu.VMEM((TOKENS // STRETCH, STRETCH, 2 * D), jnp.bfloat16),
            pltpu.VMEM((HALF // STRETCH, STRETCH, D), jnp.bfloat16),
            pltpu.VMEM((4, ROWS, D), jnp.bfloat16),
            pltpu.VMEM((24, ROWS, D), jnp.bfloat16),
            pltpu.VMEM((24, D, 384), jnp.bfloat16),
            pltpu.VMEM((ROWS, 384), jnp.float32),
            pltpu.VMEM((HALF, D), jnp.float32),
            pltpu.VMEM((HALF, D), jnp.float32),
            pltpu.VMEM((HALF, D), jnp.float32),
            dma((3, 3)), dma((4, 3)),
            dma((2, 4, 4)), dma((2, 4, 4)),
            dma((8,)), dma((8,)),
            dma((8, 3)), dma((8,)), dma((3, 2)),
            dma((8,)), dma((8,)),
            dma((4,)), dma((3,)),
            dma((2, 3)), dma((2, 3)),
            dma((2, 3)), dma((2, 3)),
            dma((5, 3)), dma((5, 3)),
        ],
        compiler_params=pltpu.CompilerParams(
            collective_id=0, has_side_effects=True, vmem_limit_bytes=60 * 1024 * 1024),
        cost_estimate=pl.CostEstimate(
            flops=2_400_000_000, bytes_accessed=4_000_000, transcendentals=3_000_000),
    )(*(a.reshape(PER, STRETCH, 384) for a in (query, keys, values)), shot_ids.reshape(TOKENS // SUB, SUB), routes.T, out_weight.reshape(3, D, 3072))


def solution(mesh):
    placed = (P("seq", "head"), P("seq", "head"), P("seq", "head"), P(), P(), P("head", None))
    return jax.shard_map(
        shards, mesh=mesh, in_specs=placed, out_specs=P("seq", "head"), check_vma=False
    )
```

```python
import math

import jax
import jax.numpy as jnp
from jax import lax
from jax.experimental import pallas as pl
from jax.experimental.pallas import tpu as pltpu
from jax.sharding import PartitionSpec as P

D = 128
ROWS = 256
STRETCH = 64
ROUTES = 8
SEQ = 64
PER = ROWS // STRETCH
NY = 8
SPARE = 3
TOKENS = SEQ * ROWS
HALF = 4 * ROWS
SUB = 128
REACH = 1024
WINDOW = SUB + 2 * REACH
NEGATIVE = -1e30
FACTOR = D ** -0.5 * math.log2(math.e)
NT = (((1,), (1,)), ((), ()))
RIGHT, LEFT = 0, 1


def kernel(q_ref, k_ref, v_ref, ids_hbm, routes_hbm, w_ref, out_ref,
           ids_ref, routes_ref, small, kv, qbuf, att, gbuf, wbuf, total, top_s, mass_s, acc_s,
           qs, qr, ring_s, ring_r, sib_s, sib_r, hand_s, hand_r, spare_s, w_s, w_r, back_s, back_r,
           xs, xr, x2s, x2r, xsib_s, xsib_r):
    p = lax.axis_index("seq")
    hd = lax.axis_index("head")
    z, y = p // NY, p % NY
    x, c = hd // 2, hd % 2
    sibling = (p, 2 * x + 1 - c)

    def remote(src, dst, send, recv, device):
        return pltpu.make_async_remote_copy(
            src_ref=src, dst_ref=dst, send_sem=send, recv_sem=recv,
            device_id=device, device_id_type=pl.DeviceIdType.MESH)

    def arrived(ref, sem):
        pltpu.make_async_copy(ref, ref, sem).wait()

    def sent(ref, sem):
        pltpu.make_async_copy(ref, ref, sem).wait()

    ids_copy = pltpu.make_async_copy(ids_hbm, ids_ref, small.at[0])
    routes_copy = pltpu.make_async_copy(routes_hbm, routes_ref, small.at[1])
    ids_copy.start()
    routes_copy.start()

    barrier = pltpu.get_barrier_semaphore()
    peers = [sibling]
    for d in range(1, NY):
        there = z * NY + (y + d) % NY
        peers += [(there, hd), (there, 2 * x + 1 - c)]
    zr, zl = (z + 1) % 8 * NY + y, (z + 7) % 8 * NY + y
    peers += [(zr, hd), (zl, hd)]
    for d in range(1, 4):
        xo = (x + d) % 4
        peers += [(p, 2 * xo), (p, 2 * xo + 1)]
    for device in peers:
        pl.semaphore_signal(barrier, inc=1, device_id=device,
                            device_id_type=pl.DeviceIdType.MESH)
    pl.semaphore_wait(barrier, len(peers))

    core = y // 4
    row0, q0 = p * PER, y % 4 * PER
    own_k = kv.at[pl.ds(row0, PER), :, 0:D]
    own_v = kv.at[pl.ds(row0, PER), :, D:2 * D]
    own_q = qbuf.at[pl.ds(q0, PER)]
    turned = (y + 10 - 4 * c) % 8 // 4

    def to_column(n, t, src, dst):
        i = n + turned * (2 - 2 * n)
        h = 4 * c + i
        own = h == y
        part = src.at[:, :, pl.ds(pl.multiple_of(i * D, D), D)]

        @pl.when(jnp.logical_not(own))
        def _():
            remote(part, dst, qs.at[n, t], qr.at[y % 4, t], (z * NY + h, 2 * x + core)).start()

        @pl.when(own)
        def _():
            pltpu.make_async_copy(part, dst, qr.at[y % 4, t]).start()

    def left_for_column(n, t):
        h = 4 * c + n + turned * (2 - 2 * n)

        @pl.when(h != y)
        def _():
            sent(qbuf.at[pl.ds(0, PER)], qs.at[n, t])

    def queries_to_columns():
        for n in range(3):
            to_column(n, 2, q_ref, own_q)

    for n in range(3):
        to_column(n, 0, k_ref, own_k)
        to_column(n, 1, v_ref, own_v)

    w_here = wbuf.at[pl.ds(3 * hd, 3)]

    def w_part(of):
        return w_ref.at[:, :, pl.ds(pl.multiple_of(of * 384, 384), 384)]

    for d in range(1, 8):
        other = (hd + d) % 8
        remote(w_part(other), w_here, w_s.at[d], w_r.at[d], (p, other)).start()
    w_own = pltpu.make_async_copy(w_part(hd), w_here, w_s.at[0])
    w_own.start()

    def nth(k, core_of):
        return (y + 2 * ((y // 4 + core_of) % 2) + (0, 1, 3, 2)[k]) % 4

    def piece_of(row, core_of, n, cut=(0, PER)):
        return kv.at[pl.ds((row * NY + 4 * core_of + n) * PER + cut[0], cut[1])]

    def half_of(row, core_of):
        return kv.at[pl.ds((row * NY + 4 * core_of) * PER, 4 * PER)]

    def to_sibling(o, row, n, cut=(0, PER)):
        ref = piece_of(row, c, n, cut)
        return remote(ref, ref, sib_s.at[o], sib_r.at[o], sibling)

    def hop(way, step, ref, n):
        return remote(ref, ref, ring_s.at[way, step, n], ring_r.at[way, step, n],
                      (zr if way == RIGHT else zl, hd))

    lean = jnp.logical_xor(core == c, y % 4 == 0)
    whole, lower, upper = (0, PER), (0, PER // 2), (PER // 2, PER // 2)

    def ring_part(n, fn):
        @pl.when(n != SPARE)
        def _():
            fn(whole)

        @pl.when(jnp.logical_and(n == SPARE, jnp.logical_not(lean)))
        def _():
            fn(lower)

    def origin(way, step):
        return (z + 8 - 1 - step) % 8 if way == RIGHT else (z + 1 + step) % 8

    def slot(way, step):
        return 1 + 2 * step + way if step < 3 else 7

    def goes(k, way, step):
        return step < 3 or k // 2 == way

    def shot(b):
        start = (z * 2 + c) * (HALF // SUB) + b
        pieces = [(start + n + TOKENS // SUB - REACH // SUB) % (TOKENS // SUB)
                  for n in range(WINDOW // SUB)]
        rows = [pl.ds(n * (SUB // STRETCH), SUB // STRETCH) for n in pieces]
        at = pl.ds(pl.multiple_of(b * SUB, SUB), SUB)
        q = qbuf[pl.ds(b * (SUB // STRETCH), SUB // STRETCH)].reshape(SUB, D)
        mine = jnp.broadcast_to(ids_ref[pl.ds(start, 1), :], (SUB, SUB)).T
        scores = []
        peak = None
        for n, r in zip(pieces, rows):
            s = lax.dot_general(q, kv[r, :, 0:D].reshape(SUB, D), NT, preferred_element_type=jnp.float32)
            s = jnp.where(mine == ids_ref[pl.ds(n, 1), :], s, NEGATIVE)
            peak = s if peak is None else jnp.maximum(peak, s)
            scores.append(s)
        top = jnp.max(peak, axis=1, keepdims=True)
        added = None
        acc = None
        for s, r in zip(scores, rows):
            e = jnp.exp2((s - top) * FACTOR)
            added = e if added is None else added + e
            one = jnp.dot(e.astype(jnp.bfloat16), kv[r, :, D:2 * D].reshape(SUB, D), preferred_element_type=jnp.float32)
            acc = one if acc is None else acc + one
        mass = jnp.sum(added, axis=1, keepdims=True)
        top_s[at, :] = jnp.broadcast_to(top, (SUB, D))
        mass_s[at, :] = jnp.broadcast_to(mass, (SUB, D))
        acc_s[at, :] = acc

    def routed(b):
        ats = [pl.ds(pl.multiple_of(b * ROWS, ROWS) + g * STRETCH, STRETCH) for g in range(PER)]
        stretch = (z * 2 + c) * 16 + b * PER
        rows = [[routes_ref[j, stretch + g] for j in range(ROUTES)] for g in range(PER)]
        scores = []
        for g in range(PER):
            keys = jnp.concatenate([kv[r, :, 0:D] for r in rows[g]], axis=0)
            scores.append(lax.dot_general(qbuf[b * PER + g], keys, NT,
                                          preferred_element_type=jnp.float32))
        before = [top_s[at, :] for at in ats]
        tops = [jnp.maximum(t, jnp.max(s, axis=1, keepdims=True)) for t, s in zip(before, scores)]
        exps = [jnp.exp2((s - t[:, :1]) * FACTOR) for s, t in zip(scores, tops)]
        keeps = [jnp.exp2((o - t) * FACTOR) for o, t in zip(before, tops)]
        sums = []
        for g in range(PER):
            vals = jnp.concatenate([kv[r, :, D:2 * D] for r in rows[g]], axis=0)
            sums.append(jnp.dot(exps[g].astype(jnp.bfloat16), vals,
                                preferred_element_type=jnp.float32))
        for g in range(PER):
            mass = keeps[g] * mass_s[ats[g], :] + jnp.sum(exps[g], axis=1, keepdims=True)
            summed = keeps[g] * acc_s[ats[g], :] + sums[g]
            att[b, g * STRETCH:(g + 1) * STRETCH, :] = (summed / mass).astype(jnp.bfloat16)

    def back(b):
        to = 4 * c + b
        return gbuf.at[6 * x + 3 * core + y % 4], (z * NY + to, 2 * x + core), to == y

    ids_copy.wait()
    routes_copy.wait()

    @pl.when(y % 4 < SPARE)
    def _():
        def own(k):
            n = nth(k, c)
            for t in range(2):
                arrived(qbuf.at[pl.ds(0, PER)], qr.at[n, t])

            def begin(cut):
                ref = piece_of(z, c, n, cut)
                hop(RIGHT, 0, ref, n).start()
                hop(LEFT, 0, ref, n).start()

            ring_part(n, begin)
            to_sibling(0, z, n).start()

        def pass_on(step, k):
            n = nth(k, c)

            def carry(cut):
                for way in (RIGHT, LEFT):
                    if goes(k, way, step):
                        row = origin(way, step)
                        ref = piece_of(row, c, n, cut)
                        arrived(ref, ring_r.at[way, step, n])
                        if step < 3 and goes(k, way, step + 1):
                            hop(way, step + 1, ref, n).start()
                        to_sibling(slot(way, step), row, n, cut).start()

            ring_part(n, carry)

        def handed(step):
            def take(cut):
                for way in (RIGHT, LEFT)[:2 if step < 3 else 1]:
                    row = origin(way, step)
                    arrived(piece_of(row, c, SPARE, cut), hand_r.at[slot(way, step)])
                    to_sibling(slot(way, step), row, SPARE, cut).start()

            @pl.when(lean)
            def _():
                take(whole)

            @pl.when(jnp.logical_not(lean))
            def _():
                take(upper)

        def from_sibling(o, row):
            arrived(half_of(row, 1 - c), sib_r.at[o])

        own(0)
        own(1)
        pass_on(0, 0)
        own(2)
        pass_on(0, 1)
        own(3)
        queries_to_columns()
        pass_on(0, 2)
        pass_on(0, 3)
        for k in range(4):
            pass_on(1, k)
        handed(0)
        for n in range(4):
            arrived(qbuf.at[pl.ds(0, PER)], qr.at[n, 2])
        from_sibling(0, z)
        from_sibling(slot(RIGHT, 0), origin(RIGHT, 0))
        from_sibling(slot(LEFT, 0), origin(LEFT, 0))
        for k in range(4):
            pass_on(2, k)
            pl.loop(2 * k, 2 * k + 2)(shot)
        handed(1)
        handed(2)
        for k in range(4):
            pass_on(3, k)
        handed(3)
        for step in (1, 2):
            for way in (RIGHT, LEFT):
                from_sibling(slot(way, step), origin(way, step))
        from_sibling(7, origin(RIGHT, 3))

        for k in range(4):
            b = (k + y) % 4
            routed(b)
            piece, device, mine = back(b)

            @pl.when(jnp.logical_not(mine))
            def _():
                remote(att.at[b], piece, back_s.at[k], back_r.at[y % 4], device).start()

            @pl.when(mine)
            def _():
                pltpu.make_async_copy(att.at[b], piece, back_r.at[y % 4]).start()

    def each(fn):
        for i in range(3):
            near = jnp.logical_xor(core == c, i == 0)

            @pl.when(near)
            def _():
                fn(i, whole)

            @pl.when(jnp.logical_not(near))
            def _():
                fn(i, upper)

    def spare_piece(row, i, cut):
        return kv.at[pl.ds((row * NY + i) * PER + cut[0], cut[1])]

    def spare_goes(i, way, step):
        return step < 3 or i % 2 == way

    def hand(o, row, i, cut):
        return remote(spare_piece(row, i, cut), kv.at[pl.ds((row * NY + y) * PER + cut[0], cut[1])],
                      hand_s.at[o, i], hand_r.at[o], (z * NY + 4 * c + i, 2 * x + core))

    @pl.when(y % 4 == SPARE)
    def _():
        def fetch(i, cut):
            at = spare_piece(z, i, cut)
            return [pltpu.make_async_copy(src.at[cut[0]:cut[0] + cut[1], :, i * D:(i + 1) * D],
                                          at.at[:, :, t * D:(t + 1) * D],
                                          spare_s.at[i, t]) for t, src in enumerate((k_ref, v_ref))]

        def begin(i, cut):
            for copy in fetch(i, cut):
                copy.start()

        def launch(i, cut):
            for copy in fetch(i, cut):
                copy.wait()
            for way in (RIGHT, LEFT):
                hop(way, 0, spare_piece(z, i, cut), i).start()

        each(begin)
        each(launch)
        for step in range(4):
            def carry(i, cut):
                for way in (RIGHT, LEFT):
                    if spare_goes(i, way, step):
                        row = origin(way, step)
                        ref = spare_piece(row, i, cut)
                        arrived(ref, ring_r.at[way, step, i])
                        if step < 3 and spare_goes(i, way, step + 1):
                            hop(way, step + 1, ref, i).start()
                        hand(slot(way, step), row, i, cut).start()

            each(carry)
            if step == 0:
                for n in range(3):
                    left_for_column(n, 0)
                    left_for_column(n, 1)
                queries_to_columns()

    xright, xleft = (p, (x + 1) % 4 * 2 + c), (p, (x + 3) % 4 * 2 + c)
    beside = (xright, xleft)
    parts = (pl.ds(0, ROWS // 2), pl.ds(ROWS // 2, ROWS // 2))
    far = (x + 2) % 4
    came = ((x + 3) % 4, (x + 1) % 4)

    def from_columns(i):
        ref = gbuf.at[3 * hd + i]
        arrived(ref, back_r.at[i])
        for way in (RIGHT, LEFT):
            remote(ref, ref, xs.at[way, i], xr.at[way, i], beside[way]).start()
        remote(ref, ref, xsib_s.at[0, i], xsib_r.at[0, i], sibling).start()

    def from_beside(i):
        for way in (RIGHT, LEFT):
            at = 3 * (2 * came[way] + c) + i
            ref, cut = gbuf.at[at], gbuf.at[at, parts[way]]
            arrived(ref, xr.at[way, i])
            remote(cut, cut, x2s.at[way, i], x2r.at[way, i], beside[way]).start()
            remote(ref, ref, xsib_s.at[1 + way, i], xsib_r.at[1 + way, i], sibling).start()

    def from_far(i):
        for way in (RIGHT, LEFT):
            cut = gbuf.at[3 * (2 * far + c) + i, parts[way]]
            arrived(cut, x2r.at[way, i])
            remote(cut, cut, xsib_s.at[3 + way, i], xsib_r.at[3 + way, i], sibling).start()

    def project(core_of, i):
        left = jnp.concatenate([gbuf[3 * (2 * n + core_of) + i] for n in range(4)], axis=1)
        right = jnp.concatenate([wbuf[3 * (2 * n + core_of) + i] for n in range(4)], axis=0)
        total[...] += jnp.dot(left, right, preferred_element_type=jnp.float32)

    def project_own(i):
        project(c, i)

    def project_sibling(i):
        for o, xo in ((0, x), (1, came[RIGHT]), (2, came[LEFT])):
            arrived(gbuf.at[3 * (2 * xo + 1 - c) + i], xsib_r.at[o, i])
        for way in (RIGHT, LEFT):
            arrived(gbuf.at[3 * (2 * far + 1 - c) + i, parts[way]], xsib_r.at[3 + way, i])
        project(1 - c, i)

    def in_turn(n, stage):
        i = (y + 4 - n) % 4

        @pl.when(i < 3)
        def _():
            stage(i)

    total[...] = jnp.zeros((ROWS, 384), jnp.float32)
    w_own.wait()
    for d in range(1, 8):
        arrived(w_here, w_r.at[d])
    for turn in range(6):
        for late, stage in enumerate((from_columns, from_beside, from_far)):
            if 0 <= turn - late < 4:
                in_turn(turn - late, stage)
    for turn in range(4):
        in_turn(turn, project_own)
    for turn in range(4):
        in_turn(turn, project_sibling)

    out_ref[...] = total[...].astype(jnp.bfloat16)

    for i in range(3):
        for way in (RIGHT, LEFT):
            sent(gbuf.at[0], xs.at[way, i])
            sent(gbuf.at[0, parts[way]], x2s.at[way, i])
            sent(gbuf.at[0, parts[way]], xsib_s.at[3 + way, i])
        for o in range(3):
            sent(gbuf.at[0], xsib_s.at[o, i])
    for d in range(1, 8):
        sent(w_here, w_s.at[d])
    for n in range(3):
        left_for_column(n, 2)

    @pl.when(y % 4 < SPARE)
    def _():
        for n in range(3):
            left_for_column(n, 0)
            left_for_column(n, 1)
        for k in range(4):
            n = nth(k, c)

            def gone(cut):
                for step in range(4):
                    for way in (RIGHT, LEFT):
                        if goes(k, way, step):
                            hop(way, step, piece_of(z, c, n, cut), n).wait_send()

            ring_part(n, gone)
        for o in range(8):
            sent(half_of(z, c), sib_s.at[o])
        for k in range(4):
            piece, device, mine = back((k + y) % 4)

            @pl.when(jnp.logical_not(mine))
            def _():
                sent(att.at[0], back_s.at[k])

    @pl.when(y % 4 == SPARE)
    def _():
        def gone(i, cut):
            for step in range(4):
                for way in (RIGHT, LEFT):
                    if spare_goes(i, way, step):
                        hop(way, step, spare_piece(z, i, cut), i).wait_send()
                        hand(slot(way, step), z, i, cut).wait_send()

        each(gone)


def shards(query, keys, values, shot_ids, routes, out_weight):
    vmem, hbm = pl.BlockSpec(memory_space=pltpu.VMEM), pl.BlockSpec(memory_space=pl.ANY)
    dma = pltpu.SemaphoreType.DMA
    return pl.pallas_call(
        kernel,
        out_shape=jax.ShapeDtypeStruct((ROWS, 384), jnp.bfloat16),
        in_specs=[hbm] * 6,
        out_specs=vmem,
        scratch_shapes=[
            pltpu.VMEM((TOKENS // SUB, SUB), jnp.int32),
            pltpu.SMEM((ROUTES, TOKENS // STRETCH), jnp.int32),
            dma((2,)),
            pltpu.VMEM((TOKENS // STRETCH, STRETCH, 2 * D), jnp.bfloat16),
            pltpu.VMEM((HALF // STRETCH, STRETCH, D), jnp.bfloat16),
            pltpu.VMEM((4, ROWS, D), jnp.bfloat16),
            pltpu.VMEM((24, ROWS, D), jnp.bfloat16),
            pltpu.VMEM((24, D, 384), jnp.bfloat16),
            pltpu.VMEM((ROWS, 384), jnp.float32),
            pltpu.VMEM((HALF, D), jnp.float32),
            pltpu.VMEM((HALF, D), jnp.float32),
            pltpu.VMEM((HALF, D), jnp.float32),
            dma((3, 3)), dma((4, 3)),
            dma((2, 4, 4)), dma((2, 4, 4)),
            dma((8,)), dma((8,)),
            dma((8, 3)), dma((8,)), dma((3, 2)),
            dma((8,)), dma((8,)),
            dma((4,)), dma((3,)),
            dma((2, 3)), dma((2, 3)),
            dma((2, 3)), dma((2, 3)),
            dma((5, 3)), dma((5, 3)),
        ],
        compiler_params=pltpu.CompilerParams(
            collective_id=0, has_side_effects=True, vmem_limit_bytes=60 * 1024 * 1024),
        cost_estimate=pl.CostEstimate(
            flops=2_400_000_000, bytes_accessed=4_000_000, transcendentals=3_000_000),
    )(*(a.reshape(PER, STRETCH, 384) for a in (query, keys, values)), shot_ids.reshape(TOKENS // SUB, SUB), routes.T, out_weight.reshape(3, D, 3072))


def solution(mesh):
    placed = (P("seq", "head"), P("seq", "head"), P("seq", "head"), P(), P(), P("head", None))
    return jax.shard_map(
        shards, mesh=mesh, in_specs=placed, out_specs=P("seq", "head"), check_vma=False
    )
```

```python
import math

import jax
import jax.numpy as jnp
from jax import lax
from jax.experimental import pallas as pl
from jax.experimental.pallas import tpu as pltpu
from jax.sharding import PartitionSpec as P

D = 128
ROWS = 256
STRETCH = 64
ROUTES = 8
SEQ = 64
PER = ROWS // STRETCH
NY = 8
SPARE = 3
TOKENS = SEQ * ROWS
HALF = 4 * ROWS
SUB = 128
REACH = 1024
WINDOW = SUB + 2 * REACH
NEGATIVE = -1e30
FACTOR = D ** -0.5 * math.log2(math.e)
NT = (((1,), (1,)), ((), ()))
RIGHT, LEFT = 0, 1


def kernel(q_ref, k_ref, v_ref, ids_hbm, routes_hbm, w_ref, out_ref,
           ids_ref, routes_ref, small, kv, qbuf, att, gbuf, wbuf, total, top_s, mass_s, acc_s,
           qs, qr, ring_s, ring_r, sib_s, sib_r, hand_s, hand_r, spare_s, w_s, w_r, back_s, back_r,
           xs, xr, x2s, x2r, xsib_s, xsib_r):
    p = lax.axis_index("seq")
    hd = lax.axis_index("head")
    z, y = p // NY, p % NY
    x, c = hd // 2, hd % 2
    sibling = (p, 2 * x + 1 - c)

    def remote(src, dst, send, recv, device):
        return pltpu.make_async_remote_copy(
            src_ref=src, dst_ref=dst, send_sem=send, recv_sem=recv,
            device_id=device, device_id_type=pl.DeviceIdType.MESH)

    def arrived(ref, sem):
        pltpu.make_async_copy(ref, ref, sem).wait()

    def sent(ref, sem):
        pltpu.make_async_copy(ref, ref, sem).wait()

    ids_copy = pltpu.make_async_copy(ids_hbm, ids_ref, small.at[0])
    routes_copy = pltpu.make_async_copy(routes_hbm, routes_ref, small.at[1])
    ids_copy.start()
    routes_copy.start()

    @pl.when(y == 4 * c + y % 4)
    def _():
        @pl.when(y % 4 < SPARE)
        def _():
            lanes = pl.ds(pl.multiple_of(y % 4 * D, D), D)
            for t, (src, dst) in enumerate((
                    (k_ref, kv.at[pl.ds(p * PER, PER), :, 0:D]),
                    (v_ref, kv.at[pl.ds(p * PER, PER), :, D:2 * D]),
                    (q_ref, qbuf.at[pl.ds(y % 4 * PER, PER)]))):
                pltpu.make_async_copy(src.at[:, :, lanes], dst, qr.at[y % 4, t]).start()

    barrier = pltpu.get_barrier_semaphore()
    peers = [sibling]
    for d in range(1, NY):
        there = z * NY + (y + d) % NY
        peers += [(there, hd), (there, 2 * x + 1 - c)]
    zr, zl = (z + 1) % 8 * NY + y, (z + 7) % 8 * NY + y
    peers += [(zr, hd), (zl, hd)]
    for d in range(1, 4):
        xo = (x + d) % 4
        peers += [(p, 2 * xo), (p, 2 * xo + 1)]
    for device in peers:
        pl.semaphore_signal(barrier, inc=1, device_id=device,
                            device_id_type=pl.DeviceIdType.MESH)
    pl.semaphore_wait(barrier, len(peers))

    core = y // 4
    row0, q0 = p * PER, y % 4 * PER
    own_k = kv.at[pl.ds(row0, PER), :, 0:D]
    own_v = kv.at[pl.ds(row0, PER), :, D:2 * D]
    own_q = qbuf.at[pl.ds(q0, PER)]
    turned = (y + 10 - 4 * c) % 8 // 4

    def to_column(n, t, src, dst):
        i = n + turned * (2 - 2 * n)
        h = 4 * c + i
        own = h == y
        part = src.at[:, :, pl.ds(pl.multiple_of(i * D, D), D)]

        @pl.when(jnp.logical_not(own))
        def _():
            remote(part, dst, qs.at[n, t], qr.at[y % 4, t], (z * NY + h, 2 * x + core)).start()

    def left_for_column(n, t):
        h = 4 * c + n + turned * (2 - 2 * n)

        @pl.when(h != y)
        def _():
            sent(qbuf.at[pl.ds(0, PER)], qs.at[n, t])

    def queries_to_columns():
        for n in range(3):
            to_column(n, 2, q_ref, own_q)

    for n in range(3):
        to_column(n, 0, k_ref, own_k)
        to_column(n, 1, v_ref, own_v)

    w_here = wbuf.at[pl.ds(3 * hd, 3)]

    def w_part(of):
        return w_ref.at[:, :, pl.ds(pl.multiple_of(of * 384, 384), 384)]

    for d in range(1, 8):
        other = (hd + d) % 8
        remote(w_part(other), w_here, w_s.at[d], w_r.at[d], (p, other)).start()
    w_own = pltpu.make_async_copy(w_part(hd), w_here, w_s.at[0])
    w_own.start()

    def nth(k, core_of):
        return (y + 2 * ((y // 4 + core_of) % 2) + (0, 1, 3, 2)[k]) % 4

    def piece_of(row, core_of, n, cut=(0, PER)):
        return kv.at[pl.ds((row * NY + 4 * core_of + n) * PER + cut[0], cut[1])]

    def half_of(row, core_of):
        return kv.at[pl.ds((row * NY + 4 * core_of) * PER, 4 * PER)]

    def to_sibling(o, row, n, cut=(0, PER)):
        ref = piece_of(row, c, n, cut)
        return remote(ref, ref, sib_s.at[o], sib_r.at[o], sibling)

    def hop(way, step, ref, n):
        return remote(ref, ref, ring_s.at[way, step, n], ring_r.at[way, step, n],
                      (zr if way == RIGHT else zl, hd))

    lean = jnp.logical_xor(core == c, y % 4 == 0)
    whole, lower, upper = (0, PER), (0, PER // 2), (PER // 2, PER // 2)

    def ring_part(n, fn):
        @pl.when(n != SPARE)
        def _():
            fn(whole)

        @pl.when(jnp.logical_and(n == SPARE, jnp.logical_not(lean)))
        def _():
            fn(lower)

    def origin(way, step):
        return (z + 8 - 1 - step) % 8 if way == RIGHT else (z + 1 + step) % 8

    def slot(way, step):
        return 1 + 2 * step + way if step < 3 else 7

    def goes(k, way, step):
        return step < 3 or k // 2 == way

    def shot(b):
        start = (z * 2 + c) * (HALF // SUB) + b
        pieces = [(start + n + TOKENS // SUB - REACH // SUB) % (TOKENS // SUB)
                  for n in range(WINDOW // SUB)]
        rows = [pl.ds(n * (SUB // STRETCH), SUB // STRETCH) for n in pieces]
        at = pl.ds(pl.multiple_of(b * SUB, SUB), SUB)
        q = qbuf[pl.ds(b * (SUB // STRETCH), SUB // STRETCH)].reshape(SUB, D)
        mine = jnp.broadcast_to(ids_ref[pl.ds(start, 1), :], (SUB, SUB)).T
        scores = []
        peak = None
        for n, r in zip(pieces, rows):
            s = lax.dot_general(q, kv[r, :, 0:D].reshape(SUB, D), NT, preferred_element_type=jnp.float32)
            s = jnp.where(mine == ids_ref[pl.ds(n, 1), :], s, NEGATIVE)
            peak = s if peak is None else jnp.maximum(peak, s)
            scores.append(s)
        top = jnp.max(peak, axis=1, keepdims=True)
        added = None
        acc = None
        for s, r in zip(scores, rows):
            e = jnp.exp2((s - top) * FACTOR)
            added = e if added is None else added + e
            one = jnp.dot(e.astype(jnp.bfloat16), kv[r, :, D:2 * D].reshape(SUB, D), preferred_element_type=jnp.float32)
            acc = one if acc is None else acc + one
        mass = jnp.sum(added, axis=1, keepdims=True)
        top_s[at, :] = jnp.broadcast_to(top, (SUB, D))
        mass_s[at, :] = jnp.broadcast_to(mass, (SUB, D))
        acc_s[at, :] = acc

    def routed(b):
        ats = [pl.ds(pl.multiple_of(b * ROWS, ROWS) + g * STRETCH, STRETCH) for g in range(PER)]
        stretch = (z * 2 + c) * 16 + b * PER
        rows = [[routes_ref[j, stretch + g] for j in range(ROUTES)] for g in range(PER)]
        scores = []
        for g in range(PER):
            keys = jnp.concatenate([kv[r, :, 0:D] for r in rows[g]], axis=0)
            scores.append(lax.dot_general(qbuf[b * PER + g], keys, NT,
                                          preferred_element_type=jnp.float32))
        before = [top_s[at, :] for at in ats]
        tops = [jnp.maximum(t, jnp.max(s, axis=1, keepdims=True)) for t, s in zip(before, scores)]
        exps = [jnp.exp2((s - t[:, :1]) * FACTOR) for s, t in zip(scores, tops)]
        keeps = [jnp.exp2((o - t) * FACTOR) for o, t in zip(before, tops)]
        sums = []
        for g in range(PER):
            vals = jnp.concatenate([kv[r, :, D:2 * D] for r in rows[g]], axis=0)
            sums.append(jnp.dot(exps[g].astype(jnp.bfloat16), vals,
                                preferred_element_type=jnp.float32))
        for g in range(PER):
            mass = keeps[g] * mass_s[ats[g], :] + jnp.sum(exps[g], axis=1, keepdims=True)
            summed = keeps[g] * acc_s[ats[g], :] + sums[g]
            att[b, g * STRETCH:(g + 1) * STRETCH, :] = (summed / mass).astype(jnp.bfloat16)

    def back(b):
        to = 4 * c + b
        return gbuf.at[6 * x + 3 * core + y % 4], (z * NY + to, 2 * x + core), to == y

    ids_copy.wait()
    routes_copy.wait()

    @pl.when(y % 4 < SPARE)
    def _():
        def own(k):
            n = nth(k, c)
            for t in range(2):
                arrived(qbuf.at[pl.ds(0, PER)], qr.at[n, t])

            def begin(cut):
                ref = piece_of(z, c, n, cut)
                hop(RIGHT, 0, ref, n).start()
                hop(LEFT, 0, ref, n).start()

            ring_part(n, begin)
            to_sibling(0, z, n).start()

        def pass_on(step, k):
            n = nth(k, c)

            def carry(cut):
                for way in (RIGHT, LEFT):
                    if goes(k, way, step):
                        row = origin(way, step)
                        ref = piece_of(row, c, n, cut)
                        arrived(ref, ring_r.at[way, step, n])
                        if step < 3 and goes(k, way, step + 1):
                            hop(way, step + 1, ref, n).start()
                        to_sibling(slot(way, step), row, n, cut).start()

            ring_part(n, carry)

        def handed(step):
            def take(cut):
                for way in (RIGHT, LEFT)[:2 if step < 3 else 1]:
                    row = origin(way, step)
                    arrived(piece_of(row, c, SPARE, cut), hand_r.at[slot(way, step)])
                    to_sibling(slot(way, step), row, SPARE, cut).start()

            @pl.when(lean)
            def _():
                take(whole)

            @pl.when(jnp.logical_not(lean))
            def _():
                take(upper)

        def from_sibling(o, row):
            arrived(half_of(row, 1 - c), sib_r.at[o])

        own(0)
        own(1)
        pass_on(0, 0)
        own(2)
        pass_on(0, 1)
        own(3)
        pass_on(0, 2)
        pass_on(0, 3)
        queries_to_columns()
        for k in range(4):
            pass_on(1, k)
        handed(0)
        for n in range(4):
            arrived(qbuf.at[pl.ds(0, PER)], qr.at[n, 2])
        from_sibling(0, z)
        from_sibling(slot(RIGHT, 0), origin(RIGHT, 0))
        from_sibling(slot(LEFT, 0), origin(LEFT, 0))
        for k in range(4):
            pass_on(2, k)
            pl.loop(2 * k, 2 * k + 2)(shot)
        handed(1)
        handed(2)
        for k in range(4):
            pass_on(3, k)
        handed(3)
        for step in (1, 2):
            for way in (RIGHT, LEFT):
                from_sibling(slot(way, step), origin(way, step))
        from_sibling(7, origin(RIGHT, 3))

        for k in range(4):
            b = (k + y) % 4
            routed(b)
            piece, device, mine = back(b)

            @pl.when(jnp.logical_not(mine))
            def _():
                remote(att.at[b], piece, back_s.at[k], back_r.at[y % 4], device).start()

            @pl.when(mine)
            def _():
                pltpu.make_async_copy(att.at[b], piece, back_r.at[y % 4]).start()

    def each(fn):
        for i in range(3):
            near = jnp.logical_xor(core == c, i == 0)

            @pl.when(near)
            def _():
                fn(i, whole)

            @pl.when(jnp.logical_not(near))
            def _():
                fn(i, upper)

    def spare_piece(row, i, cut):
        return kv.at[pl.ds((row * NY + i) * PER + cut[0], cut[1])]

    def spare_goes(i, way, step):
        return step < 3 or i % 2 == way

    def hand(o, row, i, cut):
        return remote(spare_piece(row, i, cut), kv.at[pl.ds((row * NY + y) * PER + cut[0], cut[1])],
                      hand_s.at[o, i], hand_r.at[o], (z * NY + 4 * c + i, 2 * x + core))

    @pl.when(y % 4 == SPARE)
    def _():
        def fetch(i, cut):
            at = spare_piece(z, i, cut)
            return [pltpu.make_async_copy(src.at[cut[0]:cut[0] + cut[1], :, i * D:(i + 1) * D],
                                          at.at[:, :, t * D:(t + 1) * D],
                                          spare_s.at[i, t]) for t, src in enumerate((k_ref, v_ref))]

        def begin(i, cut):
            for copy in fetch(i, cut):
                copy.start()

        def launch(i, cut):
            for copy in fetch(i, cut):
                copy.wait()
            for way in (RIGHT, LEFT):
                hop(way, 0, spare_piece(z, i, cut), i).start()

        each(begin)
        each(launch)
        for step in range(4):
            def carry(i, cut):
                for way in (RIGHT, LEFT):
                    if spare_goes(i, way, step):
                        row = origin(way, step)
                        ref = spare_piece(row, i, cut)
                        arrived(ref, ring_r.at[way, step, i])
                        if step < 3 and spare_goes(i, way, step + 1):
                            hop(way, step + 1, ref, i).start()
                        hand(slot(way, step), row, i, cut).start()

            each(carry)
            if step == 0:
                for n in range(3):
                    left_for_column(n, 0)
                    left_for_column(n, 1)
                queries_to_columns()

    xright, xleft = (p, (x + 1) % 4 * 2 + c), (p, (x + 3) % 4 * 2 + c)
    beside = (xright, xleft)
    parts = (pl.ds(0, ROWS // 2), pl.ds(ROWS // 2, ROWS // 2))
    far = (x + 2) % 4
    came = ((x + 3) % 4, (x + 1) % 4)

    def from_columns(i):
        ref = gbuf.at[3 * hd + i]
        arrived(ref, back_r.at[i])
        for way in (RIGHT, LEFT):
            remote(ref, ref, xs.at[way, i], xr.at[way, i], beside[way]).start()
        remote(ref, ref, xsib_s.at[0, i], xsib_r.at[0, i], sibling).start()

    def from_beside(i):
        for way in (RIGHT, LEFT):
            at = 3 * (2 * came[way] + c) + i
            ref, cut = gbuf.at[at], gbuf.at[at, parts[way]]
            arrived(ref, xr.at[way, i])
            remote(cut, cut, x2s.at[way, i], x2r.at[way, i], beside[way]).start()
            remote(ref, ref, xsib_s.at[1 + way, i], xsib_r.at[1 + way, i], sibling).start()

    def from_far(i):
        for way in (RIGHT, LEFT):
            cut = gbuf.at[3 * (2 * far + c) + i, parts[way]]
            arrived(cut, x2r.at[way, i])
            remote(cut, cut, xsib_s.at[3 + way, i], xsib_r.at[3 + way, i], sibling).start()

    def project(core_of, i):
        left = jnp.concatenate([gbuf[3 * (2 * n + core_of) + i] for n in range(4)], axis=1)
        right = jnp.concatenate([wbuf[3 * (2 * n + core_of) + i] for n in range(4)], axis=0)
        total[...] += jnp.dot(left, right, preferred_element_type=jnp.float32)

    def project_own(i):
        project(c, i)

    def project_sibling(i):
        for o, xo in ((0, x), (1, came[RIGHT]), (2, came[LEFT])):
            arrived(gbuf.at[3 * (2 * xo + 1 - c) + i], xsib_r.at[o, i])
        for way in (RIGHT, LEFT):
            arrived(gbuf.at[3 * (2 * far + 1 - c) + i, parts[way]], xsib_r.at[3 + way, i])
        project(1 - c, i)

    def in_turn(n, stage):
        i = (y + 4 - n) % 4

        @pl.when(i < 3)
        def _():
            stage(i)

    total[...] = jnp.zeros((ROWS, 384), jnp.float32)
    w_own.wait()
    for d in range(1, 8):
        arrived(w_here, w_r.at[d])
    for turn in range(7):
        for late, stage in enumerate((from_columns, from_beside, from_far, project_own)):
            if 0 <= turn - late < 4:
                in_turn(turn - late, stage)
    for turn in range(4):
        in_turn(turn, project_sibling)

    out_ref[...] = total[...].astype(jnp.bfloat16)

    for i in range(3):
        for way in (RIGHT, LEFT):
            sent(gbuf.at[0], xs.at[way, i])
            sent(gbuf.at[0, parts[way]], x2s.at[way, i])
            sent(gbuf.at[0, parts[way]], xsib_s.at[3 + way, i])
        for o in range(3):
            sent(gbuf.at[0], xsib_s.at[o, i])
    for d in range(1, 8):
        sent(w_here, w_s.at[d])
    for n in range(3):
        left_for_column(n, 2)

    @pl.when(y % 4 < SPARE)
    def _():
        for n in range(3):
            left_for_column(n, 0)
            left_for_column(n, 1)
        for k in range(4):
            n = nth(k, c)

            def gone(cut):
                for step in range(4):
                    for way in (RIGHT, LEFT):
                        if goes(k, way, step):
                            hop(way, step, piece_of(z, c, n, cut), n).wait_send()

            ring_part(n, gone)
        for o in range(8):
            sent(half_of(z, c), sib_s.at[o])
        for k in range(4):
            piece, device, mine = back((k + y) % 4)

            @pl.when(jnp.logical_not(mine))
            def _():
                sent(att.at[0], back_s.at[k])

    @pl.when(y % 4 == SPARE)
    def _():
        def gone(i, cut):
            for step in range(4):
                for way in (RIGHT, LEFT):
                    if spare_goes(i, way, step):
                        hop(way, step, spare_piece(z, i, cut), i).wait_send()
                        hand(slot(way, step), z, i, cut).wait_send()

        each(gone)


def shards(query, keys, values, shot_ids, routes, out_weight):
    vmem, hbm = pl.BlockSpec(memory_space=pltpu.VMEM), pl.BlockSpec(memory_space=pl.ANY)
    dma = pltpu.SemaphoreType.DMA
    return pl.pallas_call(
        kernel,
        out_shape=jax.ShapeDtypeStruct((ROWS, 384), jnp.bfloat16),
        in_specs=[hbm] * 6,
        out_specs=vmem,
        scratch_shapes=[
            pltpu.VMEM((TOKENS // SUB, SUB), jnp.int32),
            pltpu.SMEM((ROUTES, TOKENS // STRETCH), jnp.int32),
            dma((2,)),
            pltpu.VMEM((TOKENS // STRETCH, STRETCH, 2 * D), jnp.bfloat16),
            pltpu.VMEM((HALF // STRETCH, STRETCH, D), jnp.bfloat16),
            pltpu.VMEM((4, ROWS, D), jnp.bfloat16),
            pltpu.VMEM((24, ROWS, D), jnp.bfloat16),
            pltpu.VMEM((24, D, 384), jnp.bfloat16),
            pltpu.VMEM((ROWS, 384), jnp.float32),
            pltpu.VMEM((HALF, D), jnp.float32),
            pltpu.VMEM((HALF, D), jnp.float32),
            pltpu.VMEM((HALF, D), jnp.float32),
            dma((3, 3)), dma((4, 3)),
            dma((2, 4, 4)), dma((2, 4, 4)),
            dma((8,)), dma((8,)),
            dma((8, 3)), dma((8,)), dma((3, 2)),
            dma((8,)), dma((8,)),
            dma((4,)), dma((3,)),
            dma((2, 3)), dma((2, 3)),
            dma((2, 3)), dma((2, 3)),
            dma((5, 3)), dma((5, 3)),
        ],
        compiler_params=pltpu.CompilerParams(
            collective_id=0, has_side_effects=True, vmem_limit_bytes=60 * 1024 * 1024),
        cost_estimate=pl.CostEstimate(
            flops=2_400_000_000, bytes_accessed=4_000_000, transcendentals=3_000_000),
    )(*(a.reshape(PER, STRETCH, 384) for a in (query, keys, values)), shot_ids.reshape(TOKENS // SUB, SUB), routes.T, out_weight.reshape(3, D, 3072))


def solution(mesh):
    placed = (P("seq", "head"), P("seq", "head"), P("seq", "head"), P(), P(), P("head", None))
    return jax.shard_map(
        shards, mesh=mesh, in_specs=placed, out_specs=P("seq", "head"), check_vma=False
    )
```
